32 devices in a mesh: batch: 16 (over z, y, core), seq: 2 (over x).
Axes of the slice: x: 2, y: 2, z: 4, core: 2. Of those that a mesh axis runs over, the one named last changes fastest.
Arguments:
- tokens: bfloat16 [16, 1024, 1024], P('batch', 'seq'), may hold values from -6 to 6
- segments: int32 [16, 1024], P('batch', 'seq'), may hold values from 0 to 2, as said below
- cotangent: bfloat16 [16, 1024, 1024], P('batch', 'seq'), may hold values from -6 to 6
- mixer_gain: bfloat16 [1024], P(('batch', 'seq')), may hold values from 0.5 to 1.5
- mixer_shift: bfloat16 [1024], P(('batch', 'seq')), may hold values from -1.5 to 1.5
- mixer_weight: bfloat16 [1024, 3072], P(('batch', 'seq')), may hold values from -0.1875 to 0.1875
- mixer_bias: bfloat16 [3072], P(('batch', 'seq')), may hold values from -1.5 to 1.5
- merger_weight: bfloat16 [1024, 1024], P(('batch', 'seq')), may hold values from -0.75 to 0.75
- merger_bias: bfloat16 [1024], P(('batch', 'seq')), may hold values from -1.5 to 1.5
- feeder_gain: bfloat16 [1024], P(('batch', 'seq')), may hold values from 0.5 to 1.5
- feeder_shift: bfloat16 [1024], P(('batch', 'seq')), may hold values from -1.5 to 1.5
- widen_weight: bfloat16 [1024, 4096], P(('batch', 'seq')), may hold values from -0.1875 to 0.1875
- widen_bias: bfloat16 [4096], P(('batch', 'seq')), may hold values from -1.5 to 1.5
- narrow_weight: bfloat16 [4096, 1024], P(('batch', 'seq')), may hold values from -0.09375 to 0.09375
- narrow_bias: bfloat16 [1024], P(('batch', 'seq')), may hold values from -1.5 to 1.5
Outputs:
- layer_output: bfloat16 [16, 1024, 1024], P('batch', 'seq')
- tokens_grad: bfloat16 [16, 1024, 1024], P('batch', 'seq')
- mixer_gain_grad: float32 [1024], P(('batch', 'seq'))
- mixer_shift_grad: float32 [1024], P(('batch', 'seq'))
- mixer_weight_grad: float32 [1024, 3072], P(('batch', 'seq'))
- mixer_bias_grad: float32 [3072], P(('batch', 'seq'))
- merger_weight_grad: float32 [1024, 1024], P(('batch', 'seq'))
- merger_bias_grad: float32 [1024], P(('batch', 'seq'))
- feeder_gain_grad: float32 [1024], P(('batch', 'seq'))
- feeder_shift_grad: float32 [1024], P(('batch', 'seq'))
- widen_weight_grad: float32 [1024, 4096], P(('batch', 'seq'))
- widen_bias_grad: float32 [4096], P(('batch', 'seq'))
- narrow_weight_grad: float32 [4096, 1024], P(('batch', 'seq'))
- narrow_bias_grad: float32 [1024], P(('batch', 'seq'))
The draws below stay inside these ranges and needn't reach their ends.
Inputs may be any that keep to these rules, and one draw needn't show every extreme that they name: `segments`: along each sequence the numbers start at 0 and never fall, at most three documents a sequence; the tokens that share a number form one document.
All inputs are finite; a program needn't handle non-finite values.
Results may differ from the reference program's by a relative error of at most 0.009.
Values may be sent and summed in bfloat16 or wider, within the bound.
No kernel may reach another device: no remote copies, remote signals or barrier semaphores. Data moves between devices by JAX's collectives and lax.ppermute only.
A program may use at most 320 MiB of HBM per device.

```python
import jax
import jax.numpy as jnp
from jax import lax

D = 1024
HEADS = 16
HD = 64
ROT = 16
FF = 4096
SEQ_LEN = 1024
SEQS = 1
STRETCH = 512
SEQS_ALL = 16


def draw_segments(key, part):
    key = jax.random.fold_in(key, 11)
    shortest = max(1, SEQ_LEN * 200 // 1024)
    longest = max(shortest + 1, SEQ_LEN * 2000 // 1024)
    count = SEQ_LEN // shortest + 2
    keys = jax.random.split(key, 5)
    sizes = jax.random.randint(keys[0], (SEQS_ALL, count), shortest, longest)
    leading = jax.random.randint(keys[1], (SEQS_ALL, 1), 1, longest)
    bounds = jnp.cumsum(jnp.concatenate([leading, sizes[:, 1:]], 1), 1)
    place = jnp.arange(SEQ_LEN, dtype=jnp.int32)
    numbers = jnp.sum((bounds[:, None, :] <= place[None, :, None]).astype(jnp.int32), -1)
    numbers = jnp.minimum(numbers, 2)
    groups = SEQS_ALL // SEQS
    pick = jax.random.randint(keys[2], (groups,), 0, SEQS)
    index = jnp.arange(SEQS_ALL, dtype=jnp.int32)
    chosen = index % SEQS == pick[index // SEQS]
    reach = max(2, min(STRETCH, SEQ_LEN // 4))
    opening = jax.random.randint(keys[3], (SEQS_ALL, 1), 1, reach)
    closing = SEQ_LEN - jax.random.randint(keys[4], (SEQS_ALL, 1), 1, reach)
    spanning = (place[None, :] >= opening).astype(jnp.int32) + (place[None, :] >= closing).astype(jnp.int32)
    return jnp.where(chosen[:, None], spanning, numbers).astype(jnp.int32)


def strengthened(values, stream_key, source, target, blocks, factor):
    owner, partner = [(jnp.arange(values.shape[dim]) // (values.shape[dim] // blocks)).reshape([-1 if axis == dim else 1 for axis in range(values.ndim)]) for dim in (source, target)]
    chosen = jax.random.permutation(stream_key, blocks)[partner]
    strong = (owner == chosen) | (owner == (partner + blocks // 2) % blocks)
    return jnp.where(strong, factor * values, values)


def shard_levels(rng, shape, shards, low, high):
    def one(dim, blocks):
        steps = jax.random.uniform(jax.random.fold_in(jax.random.fold_in(rng, 6), dim), (blocks,), jnp.float32, low / len(shards), high / len(shards))
        return jnp.repeat(jnp.exp(steps), shape[dim] // blocks).reshape((-1,) + (1,) * (len(shape) - dim - 1))

    level = one(*shards[0])
    for cut in shards[1:]:
        level = level * one(*cut)
    return level


def normal_values(stream_key, dims, scale, most, cuts=(), kind=jnp.bfloat16):
    values = scale * jax.random.normal(stream_key, dims, jnp.float32)
    if cuts:
        values = values * shard_levels(stream_key, dims, cuts, -0.22, 0.18)
    return jnp.clip(values, -most, most).astype(kind)


def heavy_noise(own_key, extent, scale, limit, shards, heavy, kind=jnp.bfloat16):
    array = scale * jax.random.normal(own_key, extent, jnp.float32)
    if shards:
        array = array * shard_levels(own_key, extent, shards, -0.22, 0.18)
    return jnp.clip(strengthened(array, jax.random.fold_in(own_key, 3), *heavy), -limit, limit).astype(kind)


def setup_inputs(seed: int = 0) -> dict:
    streams_of = jax.random.split(jax.random.key(seed), 16)
    tokens = heavy_noise(streams_of[0], (SEQS_ALL, SEQ_LEN, D), 1.0, 6.0, ((0, 16), (1, 2)), (0, 2, 16, 2.0))
    segments = draw_segments(jax.random.fold_in(streams_of[15], 71), 0)
    cotangent = normal_values(streams_of[2], (SEQS_ALL, SEQ_LEN, D), 1.0, 6.0, ((0, 16), (1, 2)))
    mixer_gain = jnp.clip(1.0 + 0.1 * jax.random.normal(streams_of[3], (D,), jnp.float32), 0.5, 1.5).astype(jnp.bfloat16)
    mixer_shift = normal_values(streams_of[4], (D,), 0.3, 1.5, ((0, 32),))
    mixer_weight = normal_values(streams_of[5], (D, 3 * D), D ** -0.5, 0.1875, ((0, 32),))
    mixer_bias = normal_values(streams_of[6], (3 * D,), 0.3, 1.5, ((0, 32),))
    merger_weight = normal_values(streams_of[7], (D, D), (D // 16) ** -0.5, 0.75, ((0, 32),))
    merger_bias = normal_values(streams_of[8], (D,), 0.3, 1.5, ((0, 32),))
    feeder_gain = jnp.clip(1.0 + 0.1 * jax.random.normal(streams_of[9], (D,), jnp.float32), 0.5, 1.5).astype(jnp.bfloat16)
    feeder_shift = normal_values(streams_of[10], (D,), 0.3, 1.5, ((0, 32),))
    widen_weight = normal_values(streams_of[11], (D, FF), D ** -0.5, 0.1875, ((0, 32),))
    widen_bias = normal_values(streams_of[12], (FF,), 0.3, 1.5, ((0, 32),))
    narrow_weight = normal_values(streams_of[13], (FF, D), FF ** -0.5, 0.09375, ((0, 32),))
    narrow_bias = normal_values(streams_of[14], (D,), 0.3, 1.5, ((0, 32),))
    return dict(tokens=tokens, segments=segments, cotangent=cotangent, mixer_gain=mixer_gain, mixer_shift=mixer_shift, mixer_weight=mixer_weight, mixer_bias=mixer_bias, merger_weight=merger_weight, merger_bias=merger_bias, feeder_gain=feeder_gain, feeder_shift=feeder_shift, widen_weight=widen_weight, widen_bias=widen_bias, narrow_weight=narrow_weight, narrow_bias=narrow_bias)


@jax.custom_vjp
def low(v):
    return lax.optimization_barrier(v.astype(jnp.bfloat16)).astype(jnp.float32)

@jax.custom_vjp
def low_back(v):
    return v

def low_keep(v):
    return (low(v), None)

def low_pass(kept, grad):
    return (grad,)

def back_keep(v):
    return (v, None)

def back_low(kept, grad):
    return (low(grad),)
low.defvjp(low_keep, low_pass)
low_back.defvjp(back_keep, back_low)
EPS = 1e-05
SCALE = 0.125

def matmul(left, right):
    return jnp.dot(left, right, precision=lax.Precision.HIGHEST, preferred_element_type=jnp.float32)

def normalize(rows, gain, shift):
    mean = lax.optimization_barrier(jnp.mean(rows, -1, keepdims=True))
    centered = rows - mean
    spread = lax.optimization_barrier(jnp.mean(centered * centered, -1, keepdims=True))
    return centered * lax.rsqrt(spread + EPS) * gain + shift

def angles(position):
    half = ROT // 2
    freq = 10000.0 ** (-(jnp.arange(half).astype(jnp.float32) * 2.0) / float(ROT))
    phase = position.astype(jnp.float32)[..., None] * freq
    return (jnp.cos(phase), jnp.sin(phase))

def turn(value, cosine, sine):
    half = cosine.shape[-1]
    front = value[..., :half]
    behind = value[..., half:2 * half]
    remain = value[..., 2 * half:]
    cos_b = cosine[..., None, :]
    sin_b = sine[..., None, :]
    return jnp.concatenate([front * cos_b - behind * sin_b, behind * cos_b + front * sin_b, remain], -1)

def attend(item):
    query, keys, values, seg = item
    scores = low_back(jnp.einsum('qhd,khd->hqk', query, keys, precision=lax.Precision.HIGHEST) * SCALE)
    place = jnp.arange(seg.shape[0], dtype=jnp.int32)
    allowed = ((seg[:, None] == seg[None, :]) & (place[:, None] >= place[None, :]))[None]
    masked = jnp.where(allowed, scores, -1e+30)
    top = lax.optimization_barrier(jnp.max(masked, -1, keepdims=True))
    expo = jnp.where(allowed, jnp.exp(masked - top), 0.0)
    prob = low(expo / lax.optimization_barrier(jnp.sum(expo, -1, keepdims=True)))
    return jnp.einsum('hqk,khd->qhd', prob, values, precision=lax.Precision.HIGHEST)

def layer_group(inputs, seg, params):
    m_gain, m_shift, m_weight, m_bias, o_weight, o_bias, f_gain, f_shift, u_weight, u_bias, d_weight, d_bias = params
    group, length, width = inputs.shape
    flat = inputs.reshape(-1, width)
    first = low(normalize(flat, m_gain, m_shift))
    second = low(normalize(flat, f_gain, f_shift))
    project = low_back(matmul(first, m_weight) + m_bias).reshape(group, length, 3, HEADS, HD)
    place = jnp.arange(length, dtype=jnp.int32)
    earlier = lax.optimization_barrier(jnp.sum((seg[:, None, :] < seg[:, :, None]).astype(jnp.int32), -1))
    cosine, sine = angles(place[None, :] - earlier)
    query = low(turn(project[:, :, 0], cosine, sine))
    keys = low(turn(project[:, :, 1], cosine, sine))
    values = low(project[:, :, 2])
    mixed = lax.map(jax.checkpoint(attend), (query, keys, values, seg))
    mixed = low(low_back(mixed)).reshape(-1, width)
    branch_one = low_back(matmul(mixed, o_weight) + o_bias)
    widened = low_back(matmul(second, u_weight) + u_bias)
    branch_two = low_back(matmul(low(jax.nn.gelu(widened, approximate=False)), d_weight) + d_bias)
    return (flat + branch_one + branch_two).reshape(group, length, width)

def reference(tokens, segments, cotangent, mixer_gain, mixer_shift, mixer_weight, mixer_bias, merger_weight, merger_bias, feeder_gain, feeder_shift, widen_weight, widen_bias, narrow_weight, narrow_bias):
    params = tuple((p.astype(jnp.float32) for p in (mixer_gain, mixer_shift, mixer_weight, mixer_bias, merger_weight, merger_bias, feeder_gain, feeder_shift, widen_weight, widen_bias, narrow_weight, narrow_bias)))
    group = min(SEQS_ALL, max(1, 4096 // SEQ_LEN))
    while SEQS_ALL % group:
        group = group - 1
    count = SEQS_ALL // group
    inputs = tokens.astype(jnp.float32).reshape(count, group, SEQ_LEN, D)
    segs = segments.reshape(count, group, SEQ_LEN)
    cots = cotangent.astype(jnp.float32).reshape(count, group, SEQ_LEN, D)

    def advance(total, item):
        block, seg, cot = item
        result, pull = jax.vjp(lambda a, b: layer_group(a, seg, b), block, params)
        block_grad, param_grad = pull(cot)
        total = tuple((t + g for t, g in zip(total, param_grad)))
        return (total, (result.astype(jnp.bfloat16), block_grad.astype(jnp.bfloat16)))
    start = tuple((jnp.zeros_like(p) for p in params))
    total, (results, backs) = lax.scan(advance, start, (inputs, segs, cots))
    return (results.reshape(SEQS_ALL, SEQ_LEN, D), backs.reshape(SEQS_ALL, SEQ_LEN, D), total[0], total[1], total[2], total[3], total[4], total[5], total[6], total[7], total[8], total[9], total[10], total[11])
```

```python
import functools

import jax
import jax.numpy as jnp
from jax import lax
from jax.experimental import pallas as pl
from jax.experimental.pallas import tpu as pltpu
from jax.sharding import PartitionSpec as P

HD = 64
ROT = 16
EPS = 1e-05
SCALE = 0.125
F32 = jnp.float32
BF = jnp.bfloat16


def dot(left, right, left_dim, right_dim):
    return lax.dot_general(
        left, right, (((left_dim,), (right_dim,)), ((), ())), preferred_element_type=F32
    )


def swap_batch(value, mask):
    count = lax.axis_size("batch")
    return lax.ppermute(value, "batch", [(i, i ^ mask) for i in range(count)])


def swap_seq(value, mask):
    count = lax.axis_size("seq")
    return lax.ppermute(value, "seq", [(i, i ^ mask) for i in range(count)])


def swap_member(value, mask):
    members = 2 * lax.axis_size("seq")
    count = lax.axis_size("batch") * lax.axis_size("seq")
    return lax.ppermute(
        value,
        ("batch", "seq"),
        [(i, (i // members) * members + ((i % members) ^ mask)) for i in range(count)],
    )


def put_kernel(count, first_of, *refs):
    parts, out, sem = refs[:count], refs[count], refs[count + 1]
    copies = []
    for k in range(count):
        copy = pltpu.make_async_copy(parts[k], out.at[first_of(k)], sem.at[k])
        copy.start()
        copies.append(copy)
    for copy in copies:
        copy.wait()


def assemble(parts, place):
    count = len(parts)
    return pl.pallas_call(
        functools.partial(put_kernel, count, place),
        out_shape=jax.ShapeDtypeStruct((count,) + parts[0].shape, parts[0].dtype),
        in_specs=[pl.BlockSpec(memory_space=pl.ANY)] * count,
        out_specs=pl.BlockSpec(memory_space=pl.ANY),
        scratch_shapes=[pltpu.SemaphoreType.DMA((count,))],
    )(*parts)


def gather_groups(chunk):
    groups = lax.axis_size("batch") // 2
    far = [chunk] + [swap_batch(chunk, 4 * k) for k in range(1, groups // 2)]
    near = [swap_batch(part, 2) for part in far]
    parts = [part for pair in zip(far, near) for part in pair]
    return assemble(parts, lambda k: (lax.axis_index("batch") // 2) ^ k)


def reduce_groups(value):
    groups, rows, width = value.shape
    group = lax.axis_index("batch") // 2
    near = group % 2
    far = group // 2
    halves = value.astype(BF).reshape(groups // 2, 2, rows, width)
    other = swap_batch(lax.dynamic_index_in_dim(halves, 1 - near, 1, keepdims=False), 2)
    mine = lax.dynamic_index_in_dim(halves, near, 1, keepdims=False)
    summed = (mine.astype(F32) + other.astype(F32)).astype(BF)
    total = lax.dynamic_index_in_dim(summed, far, 0, keepdims=False).astype(F32)
    for k in range(1, groups // 2):
        piece = lax.dynamic_index_in_dim(summed, far ^ k, 0, keepdims=False)
        total = total + swap_batch(piece, 4 * k).astype(F32)
    return total


def exchange_members(pieces):
    members = pieces.shape[0]
    seq = lax.axis_size("seq")
    me = (lax.axis_index("batch") % 2) * seq + lax.axis_index("seq")
    out = jnp.zeros_like(pieces)
    for k in range(members):
        piece = lax.dynamic_index_in_dim(pieces, me ^ k, 0, keepdims=True)
        got = piece if k == 0 else swap_member(piece, k)
        out = lax.dynamic_update_slice_in_dim(out, got, me ^ k, 0)
    return out


def join_tokens(value):
    seq = lax.axis_size("seq")
    here = lax.axis_index("seq")
    stretch = value.shape[1]
    if seq == 2:
        got = swap_seq(value, 1)
        out = jnp.zeros((value.shape[0], 2 * stretch, value.shape[2]), value.dtype)
        out = lax.dynamic_update_slice_in_dim(out, value, here * stretch, 1)
        whole = lax.dynamic_update_slice_in_dim(out, got, (1 - here) * stretch, 1)
    else:
        whole = lax.all_gather(value, "seq", axis=1, tiled=True)
    return jnp.concatenate([whole, swap_batch(whole, 1)], 0)


def part_tokens(value):
    seqs, length, width = value.shape
    seqs = seqs // 2
    seq = lax.axis_size("seq")
    here = lax.axis_index("seq")
    mine = value[:seqs].astype(F32) + swap_batch(value[seqs:].astype(BF), 1).astype(F32)
    stretch = length // seq
    if seq == 2:
        away = lax.dynamic_slice_in_dim(mine, (1 - here) * stretch, stretch, 1).astype(BF)
        keep = lax.dynamic_slice_in_dim(mine, here * stretch, stretch, 1)
        return keep + swap_seq(away, 1).astype(F32)
    return lax.psum_scatter(mine.astype(BF), "seq", scatter_dimension=1, tiled=True).astype(F32)


def attend_kernel(heads, block, q_ref, k_ref, v_ref, g_ref, c_ref, a_ref, b_ref, col_ref, row_ref, mixed_ref, grad_ref):
    length = q_ref.shape[0]
    half = ROT // 2
    cosine, up, down = c_ref[0], a_ref[0], b_ref[0]

    def roll(value, shift):
        if value.shape[1] % 128:
            return jnp.concatenate([value[:, -shift:], value[:, :-shift]], 1)
        return pltpu.roll(value, shift % value.shape[1], 1)

    def turn(value):
        return value * cosine - roll(value, -half) * up + roll(value, half) * down

    def turn_back(value):
        return value * cosine + roll(value, -half) * up - roll(value, half) * down

    query = (turn(q_ref[...]).astype(BF).astype(F32) * SCALE).astype(BF)
    keys = turn(k_ref[...]).astype(BF)
    values = v_ref[...].astype(BF)
    grads = g_ref[...]
    col = col_ref[0]
    row = row_ref[0]
    dq_all, dk_all, dv_all, mixed_all = [], [], [], []
    for h in range(heads):
        span = slice(h * HD, (h + 1) * HD)
        qh, kh, vh, gh = query[:, span], keys[:, span], values[:, span], grads[:, span]
        dq_parts, mixed_parts = [], []
        dk = jnp.zeros((length, HD), F32)
        dv = jnp.zeros((length, HD), F32)
        for i in range(length // block):
            n = (i + 1) * block
            rows = slice(i * block, n)
            q, g = qh[rows], gh[rows]
            k, v = kh[:n], vh[:n]
            scores = dot(q, k, 1, 1)
            place_q = lax.broadcasted_iota(jnp.int32, (block, n), 0) + i * block
            place_k = lax.broadcasted_iota(jnp.int32, (block, n), 1)
            allowed = (col[rows] == row[:, :n]) & (place_q >= place_k)
            scores = jnp.where(allowed, scores, -1e30)
            expo = jnp.exp(scores - jnp.max(scores, -1, keepdims=True))
            prob = expo * (1.0 / jnp.sum(expo, -1, keepdims=True))
            prob_b = prob.astype(BF)
            mixed_parts.append(dot(prob_b, v, 1, 0))
            prob_grad = dot(g, v, 1, 1)
            center = jnp.sum(prob * prob_grad, -1, keepdims=True)
            score_grad = (prob * (prob_grad - center)).astype(BF)
            dq_parts.append(dot(score_grad, k, 1, 0) * SCALE)
            dk_add = dot(score_grad, q, 0, 0)
            dv_add = dot(prob_b, g, 0, 0)
            if n < length:
                zeros = jnp.zeros((length - n, HD), F32)
                dk_add = jnp.concatenate([dk_add, zeros], 0)
                dv_add = jnp.concatenate([dv_add, zeros], 0)
            dk = dk + dk_add
            dv = dv + dv_add
        dq_all.append(jnp.concatenate(dq_parts, 0))
        mixed_all.append(jnp.concatenate(mixed_parts, 0))
        dk_all.append(dk)
        dv_all.append(dv)
    mixed_ref[...] = jnp.concatenate(mixed_all, 1).astype(BF)
    grad_ref[0] = turn_back(jnp.concatenate(dq_all, 1)).astype(BF)
    grad_ref[1] = turn_back(jnp.concatenate(dk_all, 1)).astype(BF)
    grad_ref[2] = jnp.concatenate(dv_all, 1).astype(BF)


def attend(project, mixed_grad, tables, segs):
    seqs, length = segs.shape
    rows, wide = project.shape
    width = wide // 3
    heads = min(2, width // HD)
    lanes = heads * HD
    steps = width // lanes
    block = min(256, length)

    parts = (project, project, project)
    ahead = steps
    if lanes % 128:
        parts = tuple(jnp.split(project, 3, 1))
        ahead = 0

    def of(part):
        return pl.BlockSpec((length, lanes), lambda s, h: (s, part * ahead + h))

    table = pl.BlockSpec((1, length, lanes), lambda s, h: (s, 0, 0))
    cost = pl.CostEstimate(
        flops=seqs * (width // HD) * length * length * HD * 12,
        bytes_accessed=rows * width * 24,
        transcendentals=seqs * (width // HD) * length * length,
    )
    return pl.pallas_call(
        functools.partial(attend_kernel, heads, block),
        grid=(seqs, steps),
        in_specs=[
            of(0),
            of(1),
            of(2),
            of(0),
            table,
            table,
            table,
            pl.BlockSpec((1, length, 1), lambda s, h: (s, 0, 0)),
            pl.BlockSpec((1, 1, length), lambda s, h: (s, 0, 0)),
        ],
        out_specs=(
            pl.BlockSpec((length, lanes), lambda s, h: (s, h)),
            pl.BlockSpec((3, length, lanes), lambda s, h: (0, s, h)),
        ),
        out_shape=(
            jax.ShapeDtypeStruct((rows, width), BF),
            jax.ShapeDtypeStruct((3, rows, width), BF),
        ),
        cost_estimate=cost,
        compiler_params=pltpu.CompilerParams(vmem_limit_bytes=56 * 1024 * 1024),
    )(*parts, mixed_grad, *tables, segs[:, :, None], segs[:, None, :])


def turn_tables(position, lanes):
    half = ROT // 2
    freq = 10000.0 ** (-(jnp.arange(half).astype(F32) * 2.0) / float(ROT))
    phase = position.astype(F32)[..., None] * freq
    cosine, sine = jnp.cos(phase), jnp.sin(phase)
    rest = phase.shape[:-1] + (HD - ROT,)
    none = jnp.zeros_like(sine)
    heads = lanes // HD

    def lay(*pieces):
        return jnp.tile(jnp.concatenate(pieces, -1), (1, 1, heads))

    return (
        lay(cosine, cosine, jnp.ones(rest, F32)),
        lay(sine, none, jnp.zeros(rest, F32)),
        lay(none, sine, jnp.zeros(rest, F32)),
    )


def local(
    tokens,
    segments,
    cotangent,
    mixer_gain,
    mixer_shift,
    mixer_weight,
    mixer_bias,
    merger_weight,
    merger_bias,
    feeder_gain,
    feeder_shift,
    widen_weight,
    widen_bias,
    narrow_weight,
    narrow_bias,
):
    seqs, stretch, width = tokens.shape
    seq = lax.axis_size("seq")
    groups = lax.axis_size("batch") // 2
    members = 2 * seq
    devices = groups * members
    length = stretch * seq
    here = lax.axis_index("seq")
    me = (lax.axis_index("batch") % 2) * seq + here
    share = mixer_weight.shape[0]
    hidden = widen_weight.shape[1]
    slim = width // members
    unit = hidden // devices
    every = ("batch", "seq")

    vectors = (
        mixer_gain,
        mixer_shift,
        mixer_bias,
        merger_bias,
        feeder_gain,
        feeder_shift,
        widen_bias,
        narrow_bias,
    )
    sizes = [v.shape[0] for v in vectors]
    cuts = [sum(sizes[: i + 1]) for i in range(len(sizes) - 1)]
    gathered = lax.all_gather(jnp.concatenate(vectors), every, axis=0, tiled=False)
    gain_m, shift_m, bias_m, bias_o, gain_f, shift_f, bias_w, bias_n = [
        v.reshape(-1).astype(F32) for v in jnp.split(gathered, cuts, 1)
    ]
    merger_all = lax.all_gather(merger_weight, every, axis=0, tiled=True)
    merger = lax.dynamic_slice_in_dim(merger_all, me * slim, slim, 0)
    mixer_pieces = mixer_weight.reshape(share, 3, members, slim).transpose(2, 0, 1, 3)
    widen_pieces = widen_weight.reshape(share, groups, members, unit).transpose(2, 0, 1, 3)
    pieces = jnp.concatenate(
        [
            mixer_pieces.reshape(members, share, 3 * slim),
            widen_pieces.reshape(members, share, groups * unit),
        ],
        -1,
    )
    chunks = exchange_members(pieces).reshape(members * share, -1)
    mixer = gather_groups(chunks[:, : 3 * slim]).reshape(width, 3 * slim)
    widen = gather_groups(chunks[:, 3 * slim :]).reshape(width, groups * unit)
    narrow = gather_groups(narrow_weight).reshape(groups * unit, width)
    bias_m_mine = lax.dynamic_index_in_dim(bias_m.reshape(3, members, slim), me, 1, keepdims=False)
    bias_w_mine = lax.dynamic_index_in_dim(bias_w.reshape(groups, members, unit), me, 1, keepdims=False)

    inputs = join_tokens(tokens)
    upstream = join_tokens(cotangent).reshape(-1, width)
    segs = join_tokens(segments[:, :, None])[:, :, 0]
    place = jnp.arange(length, dtype=jnp.int32)
    earlier = jnp.sum((segs[:, None, :] < segs[:, :, None]).astype(jnp.int32), -1)
    tables = turn_tables(place[None, :] - earlier, min(2, slim // HD) * HD)

    def centre(rows):
        mean = jnp.mean(rows, -1, keepdims=True)
        centered = rows - mean
        spread = jnp.mean(centered * centered, -1, keepdims=True)
        rstd = lax.rsqrt(spread + EPS)
        return centered * rstd, rstd

    flat = inputs.astype(F32).reshape(-1, width)
    normed, _ = centre(flat)
    first = (normed * gain_m + shift_m).astype(BF)
    second = (normed * gain_f + shift_f).astype(BF)

    project = dot(first, mixer, 1, 0) + bias_m_mine.reshape(-1)
    mixed_grad = dot(upstream, merger, 1, 1).astype(BF)
    mixed, project_grad = attend(project, mixed_grad, tables, segs)

    widened = dot(second, widen, 1, 0) + bias_w_mine.reshape(-1)
    bell = 0.5 * (1.0 + lax.erf(widened * (0.5**0.5)))
    active = (widened * bell).astype(BF)
    slope = bell + widened * jnp.exp(-0.5 * widened * widened) * (0.15915494309189535**0.5)
    narrow_grad = dot(active, upstream, 0, 0).astype(BF)
    narrow_out = reduce_groups(narrow_grad.reshape(groups, unit, width))
    widened_grad = (dot(upstream, narrow, 1, 1) * slope).astype(BF)
    widen_bias_grad = jnp.sum(widened_grad, 0, dtype=F32)
    widen_grad = dot(second, widened_grad, 0, 0).astype(BF)
    widen_sum = reduce_groups(widen_grad.reshape(groups, members * share, groups * unit))
    second_grad = dot(widened_grad, widen, 1, 1)

    partial = dot(mixed, merger, 1, 0) + dot(active, narrow, 1, 0)
    own = tokens.astype(F32)
    layer_output = (own + part_tokens(partial.reshape(2 * seqs, length, width)) + (bias_o + bias_n)).astype(BF)

    merger_grad = dot(mixed, upstream, 0, 0)
    mixer_grad = jnp.concatenate([dot(first, project_grad[i], 0, 0).astype(BF) for i in range(3)], 1)
    mixer_sum = reduce_groups(mixer_grad.reshape(groups, members * share, 3 * slim))
    first_grad = sum(
        dot(project_grad[i], mixer[:, i * slim : (i + 1) * slim], 1, 1) for i in range(3)
    )
    mixer_bias_grad = jnp.sum(project_grad, 1, dtype=F32)
    backs = exchange_members(
        jnp.concatenate([mixer_sum, widen_sum], 1).reshape(members, share, -1).astype(BF)
    ).astype(F32)
    mixer_out = backs[:, :, : 3 * slim].reshape(members, share, 3, slim).transpose(1, 2, 0, 3)
    widen_out = backs[:, :, 3 * slim :].reshape(members, share, groups, unit).transpose(1, 2, 0, 3)
    merger_full = lax.dynamic_update_slice_in_dim(
        jnp.zeros((width, width), BF), merger_grad.astype(BF), me * slim, 0
    )
    merger_out = lax.psum_scatter(merger_full, every, scatter_dimension=0, tiled=True).astype(F32)

    error = first_grad * gain_m + second_grad * gain_f
    error = part_tokens(error.reshape(2 * seqs, length, width))
    normed_own, rstd_own = centre(own)
    back = rstd_own * (
        error
        - jnp.mean(error, -1, keepdims=True)
        - normed_own * jnp.mean(error * normed_own, -1, keepdims=True)
    )
    tokens_grad = (cotangent.astype(F32) + back).astype(BF)

    def spread_out(value, lead):
        shape = (lead, members, value.size // lead)
        return lax.dynamic_update_slice_in_dim(
            jnp.zeros(shape, F32), value.reshape(lead, 1, -1), me, 1
        )

    bias_grad = jnp.sum(cotangent.astype(F32), (0, 1))
    sums = (
        jnp.sum(first_grad * normed, 0),
        jnp.sum(first_grad, 0),
        spread_out(mixer_bias_grad, 3),
        bias_grad,
        jnp.sum(second_grad * normed, 0),
        jnp.sum(second_grad, 0),
        spread_out(widen_bias_grad, groups),
        bias_grad,
    )
    packed = jnp.concatenate([v.reshape(devices, -1) for v in sums], 1)
    owned = lax.psum_scatter(packed, every, scatter_dimension=0, tiled=False)
    gain_m_out, shift_m_out, bias_m_out, bias_o_out, gain_f_out, shift_f_out, bias_w_out, bias_n_out = jnp.split(owned, cuts)
    return (
        layer_output,
        tokens_grad,
        gain_m_out,
        shift_m_out,
        mixer_out.reshape(mixer_weight.shape),
        bias_m_out,
        merger_out,
        bias_o_out,
        gain_f_out,
        shift_f_out,
        widen_out.reshape(widen_weight.shape),
        bias_w_out,
        narrow_out,
        bias_n_out,
    )


def solution(mesh):
    vector = P(("batch", "seq"))
    matrix = P(("batch", "seq"), None)
    rows = P("batch", "seq", None)
    params = (vector, vector, matrix, vector, matrix, vector, vector, vector, matrix, vector, matrix, vector)
    return jax.shard_map(
        local,
        mesh=mesh,
        in_specs=(rows, P("batch", "seq"), rows) + params,
        out_specs=(rows, rows) + params,
        check_vma=False,
    )
```

```python
import functools

import jax
import jax.numpy as jnp
from jax import lax
from jax.experimental import pallas as pl
from jax.experimental.pallas import tpu as pltpu
from jax.sharding import PartitionSpec as P

HD = 64
ROT = 16
EPS = 1e-05
SCALE = 0.125
F32 = jnp.float32
BF = jnp.bfloat16


def dot(left, right, left_dim, right_dim):
    return lax.dot_general(
        left, right, (((left_dim,), (right_dim,)), ((), ())), preferred_element_type=F32
    )


def swap_batch(value, mask):
    count = lax.axis_size("batch")
    return lax.ppermute(value, "batch", [(i, i ^ mask) for i in range(count)])


def swap_seq(value, mask):
    count = lax.axis_size("seq")
    return lax.ppermute(value, "seq", [(i, i ^ mask) for i in range(count)])


def swap_member(value, mask):
    members = 2 * lax.axis_size("seq")
    count = lax.axis_size("batch") * lax.axis_size("seq")
    return lax.ppermute(
        value,
        ("batch", "seq"),
        [(i, (i // members) * members + ((i % members) ^ mask)) for i in range(count)],
    )


def after(value, *others):
    return lax.optimization_barrier((value,) + others)[0]


def gather_groups(chunk):
    groups = lax.axis_size("batch") // 2
    far = [chunk] + [swap_batch(chunk, 4 * k) for k in range(1, groups // 2)]
    near = [swap_batch(part, 2) for part in far]
    return [part for pair in zip(far, near) for part in pair]


def sort_groups(value):
    groups = value.shape[0]
    me = lax.axis_index("batch") // 2
    bit = 1
    while bit < groups:
        paired = value.reshape((groups // (2 * bit), 2, bit) + value.shape[1:])
        flipped = jnp.concatenate([paired[:, 1:], paired[:, :1]], 1)
        value = jnp.where((me & bit) > 0, flipped, paired).reshape(value.shape)
        bit = 2 * bit
    return value


def reduce_groups(send, keep):
    got = swap_batch(send, 2)
    total = keep[0].astype(F32) + got[0].astype(F32)
    pieces = [
        (keep[k].astype(F32) + got[k].astype(F32)).astype(send.dtype) for k in range(1, send.shape[0])
    ]
    for k, piece in enumerate(pieces):
        total = total + swap_batch(piece, 4 * (k + 1)).astype(F32)
    return total


def member():
    return (lax.axis_index("batch") % 2) * lax.axis_size("seq") + lax.axis_index("seq")


def exchange_members(pieces):
    me = member()
    out = jnp.zeros_like(pieces)
    for k in range(pieces.shape[0]):
        piece = lax.dynamic_index_in_dim(pieces, me ^ k, 0, keepdims=True)
        got = piece if k == 0 else swap_member(piece, k)
        out = lax.dynamic_update_slice_in_dim(out, got, me ^ k, 0)
    return out


def gather_merger(weight):
    seq = lax.axis_size("seq")
    batch = lax.axis_size("batch")
    members = 2 * seq
    groups = batch // 2
    lows = groups // members
    share = weight.shape[0]
    every = ("batch", "seq")
    group = lax.axis_index("batch") // 2
    root = group // lows
    me = member()
    block = jnp.zeros((members,) + weight.shape, weight.dtype)
    block = lax.dynamic_update_slice_in_dim(block, weight[None], me, 0)
    for k in range(1, members):
        pairs = [
            (g * members + t, g * members + (t ^ k))
            for g in range(groups)
            for t in range(members)
            if t ^ k == g // lows
        ]
        block = lax.dynamic_update_slice_in_dim(block, lax.ppermute(weight, every, pairs)[None], me ^ k, 0)
    block = block.reshape(members * share, -1)
    found = jnp.where(me == root, block, jnp.zeros_like(block))
    for k in range(1, members):
        pairs = [
            (g * members + g // lows, (g ^ (k * lows)) * members + g // lows) for g in range(groups)
        ]
        found = found + lax.ppermute(block, every, pairs)
    whole = found[None]
    bit = 1
    while bit < lows:
        got = swap_batch(whole, 2 * bit)
        swapped = (group & bit) > 0
        whole = jnp.where(swapped, jnp.concatenate([got, whole]), jnp.concatenate([whole, got]))
        bit = 2 * bit
    return whole.reshape(-1, weight.shape[1])


def reduce_merger(grad):
    seq = lax.axis_size("seq")
    batch = lax.axis_size("batch")
    members = 2 * seq
    groups = batch // 2
    lows = groups // members
    every = ("batch", "seq")
    group = lax.axis_index("batch") // 2
    root = group // lows
    me = member()
    whole = grad.reshape((lows, -1, grad.shape[1]))
    bit = lows // 2
    while bit:
        halves = whole.reshape((2, -1) + whole.shape[1:])
        side = ((group & bit) > 0).astype(jnp.int32)
        away = lax.dynamic_index_in_dim(halves, 1 - side, 0, keepdims=False).astype(BF)
        whole = lax.dynamic_index_in_dim(halves, side, 0, keepdims=False)
        whole = whole + swap_batch(away, 2 * bit).astype(F32)
        bit = bit // 2
    block = whole[0].astype(BF)
    total = whole[0]
    for k in range(1, members):
        pairs = [
            ((g ^ (k * lows)) * members + g // lows, g * members + g // lows) for g in range(groups)
        ]
        total = total + lax.ppermute(block, every, pairs).astype(F32)
    rows = total.reshape(members, -1, grad.shape[1]).astype(BF)
    mine = lax.dynamic_index_in_dim(rows, me, 0, keepdims=False).astype(F32)
    out = jnp.where(me == root, mine, jnp.zeros_like(mine))
    for k in range(1, members):
        pairs = [
            (g * members + g // lows, g * members + ((g // lows) ^ k)) for g in range(groups)
        ]
        piece = lax.dynamic_index_in_dim(rows, me ^ k, 0, keepdims=False)
        out = out + lax.ppermute(piece, every, pairs).astype(F32)
    return out


def join_tokens(value):
    if lax.axis_size("seq") == 2:
        far = swap_seq(value, 1)
        return jnp.concatenate(
            [
                jnp.concatenate([value, far], 1),
                jnp.concatenate([swap_batch(value, 1), swap_batch(far, 1)], 1),
            ],
            0,
        )
    whole = lax.all_gather(value, "seq", axis=1, tiled=True)
    return jnp.concatenate([whole, swap_batch(whole, 1)], 0)


def part_tokens(value):
    seqs, length, _ = value.shape
    seqs = seqs // 2
    mine = value[:seqs].astype(F32) + swap_batch(value[seqs:], 1).astype(F32)
    if lax.axis_size("seq") == 2:
        stretch = length // 2
        return mine[:, :stretch] + swap_seq(mine[:, stretch:].astype(BF), 1).astype(F32)
    return lax.psum_scatter(mine.astype(BF), "seq", scatter_dimension=1, tiled=True).astype(F32)


def centre(rows):
    mean = jnp.mean(rows, -1, keepdims=True)
    centered = rows - mean
    spread = jnp.mean(centered * centered, -1, keepdims=True)
    rstd = lax.rsqrt(spread + EPS)
    return centered * rstd, rstd


def lay(parts, out_ref, group, rows):
    for k, part in enumerate(parts):
        out_ref[pl.ds(pl.multiple_of((group ^ k) * rows, rows), rows), :] = part[:rows, :]


def split_out(total_ref, send_ref, keep_ref, group, rows):
    for k in range(send_ref.shape[0]):
        keep = pl.multiple_of((group ^ (2 * k)) * rows, rows)
        send = pl.multiple_of((group ^ (2 * k + 1)) * rows, rows)
        keep_ref[k] = total_ref[pl.ds(keep, rows), :].astype(BF)
        send_ref[k] = total_ref[pl.ds(send, rows), :].astype(BF)


def add_rows(out_ref, i, row, value):
    total = jnp.sum(value, 0, keepdims=True)

    @pl.when(i == 0)
    def _():
        out_ref[row : row + 1, :] = total

    @pl.when(i > 0)
    def _():
        out_ref[row : row + 1, :] += total


def add_to(total_ref, i, value):
    @pl.when(i == 0)
    def _():
        total_ref[...] = value

    @pl.when(i > 0)
    def _():
        total_ref[...] += value


def feed_kernel(groups, info, x_ref, g_ref, gain_ref, shift_ref, bias_ref, *refs):
    widen_parts, narrow_parts = refs[:groups], refs[groups : 2 * groups]
    out_ref, e_ref, sums_ref, bsum_ref, ns_ref, nk_ref, ws_ref, wk_ref = refs[2 * groups : 2 * groups + 8]
    widen, narrow, narrow_total, widen_total = refs[2 * groups + 8 :]
    i = pl.program_id(0)
    group = info[0]
    wide_rows = widen.shape[0] // groups
    unit = narrow.shape[0] // groups

    @pl.when(i == 0)
    def _():
        lay(widen_parts, widen, group, wide_rows)
        lay(narrow_parts, narrow, group, unit)

    normed, _ = centre(x_ref[...].astype(F32))
    second = (normed * gain_ref[...] + shift_ref[...]).astype(BF)
    upstream = g_ref[...]
    widened = dot(second, widen[...], 1, 0) + bias_ref[...]
    bell = 0.5 + 0.5 * lax.erf(widened * (0.5**0.5))
    active = (widened * bell).astype(BF)
    slope = bell + widened * jnp.exp(-0.5 * widened * widened) * (0.15915494309189535**0.5)
    add_to(narrow_total, i, dot(active, upstream, 0, 0))
    out_ref[...] = dot(active, narrow[...], 1, 0).astype(BF)
    widened_grad_f = dot(upstream, narrow[...], 1, 1) * slope
    widened_grad = widened_grad_f.astype(BF)
    add_rows(bsum_ref, i, 0, widened_grad.astype(F32))
    add_to(widen_total, i, dot(second, widened_grad, 0, 0))
    second_grad = dot(widened_grad, widen[...], 1, 1)
    add_rows(sums_ref, i, 0, second_grad * normed)
    add_rows(sums_ref, i, 1, second_grad)
    e_ref[...] = (second_grad * gain_ref[...]).astype(BF)

    @pl.when(i == pl.num_programs(0) - 1)
    def _():
        split_out(narrow_total, ns_ref, nk_ref, group, unit)
        split_out(widen_total, ws_ref, wk_ref, group, wide_rows)


def whole(shape):
    return pl.BlockSpec(shape, lambda *_: (0,) * len(shape), pipeline_mode=pl.Buffered(1))


def feed(info, inputs, upstream, gain, shift, bias, widen_parts, narrow_parts):
    rows, width = inputs.shape
    groups = len(widen_parts)
    unit = narrow_parts[0].shape[0]
    hidden = groups * unit
    block = min(512, rows)
    share = width // groups
    tile = pl.BlockSpec((block, width), lambda i, _: (i, 0))
    half = groups // 2
    shapes = [(half, unit, width), (half, unit, width), (half, share, hidden), (half, share, hidden)]
    return pl.pallas_call(
        functools.partial(feed_kernel, groups),
        grid_spec=pltpu.PrefetchScalarGridSpec(
            num_scalar_prefetch=1,
            grid=(rows // block,),
            in_specs=[tile, tile, whole((1, width)), whole((1, width)), whole((1, hidden))]
            + [whole(part.shape) for part in widen_parts]
            + [whole(part.shape) for part in narrow_parts],
            out_specs=[tile, tile, whole((2, width)), whole((1, hidden))] + [whole(s) for s in shapes],
            scratch_shapes=[
                pltpu.VMEM((width, hidden), BF),
                pltpu.VMEM((hidden, width), BF),
                pltpu.VMEM((hidden, width), F32),
                pltpu.VMEM((width, hidden), F32),
            ],
        ),
        out_shape=[
            jax.ShapeDtypeStruct((rows, width), BF),
            jax.ShapeDtypeStruct((rows, width), BF),
            jax.ShapeDtypeStruct((2, width), F32),
            jax.ShapeDtypeStruct((1, hidden), F32),
        ]
        + [jax.ShapeDtypeStruct(s, BF) for s in shapes],
        cost_estimate=pl.CostEstimate(
            flops=12 * rows * width * hidden, bytes_accessed=8 * rows * width, transcendentals=2 * rows * hidden
        ),
        compiler_params=pltpu.CompilerParams(vmem_limit_bytes=60 * 1024 * 1024),
    )(info, inputs, upstream, gain, shift, bias, *widen_parts, *narrow_parts)


def project_kernel(groups, info, x_ref, g_ref, gain_ref, shift_ref, bias_ref, merger_ref, *refs):
    parts = refs[:groups]
    first_ref, project_ref, mg_ref, mixer = refs[groups:]

    @pl.when(pl.program_id(0) == 0)
    def _():
        lay(parts, mixer, info[0], mixer.shape[0] // groups)

    normed, _ = centre(x_ref[...].astype(F32))
    first = (normed * gain_ref[...] + shift_ref[...]).astype(BF)
    first_ref[...] = first
    project_ref[...] = dot(first, mixer[...], 1, 0) + bias_ref[...]
    mg_ref[...] = dot(g_ref[...], merger_ref[...], 1, 1).astype(BF)


def project_all(info, inputs, upstream, gain, shift, bias, merger, parts):
    rows, width = inputs.shape
    groups = len(parts)
    wide = parts[0].shape[1]
    slim = wide // 3
    block = min(512, rows)

    def tile(n):
        return pl.BlockSpec((block, n), lambda i, _: (i, 0))

    return pl.pallas_call(
        functools.partial(project_kernel, groups),
        grid_spec=pltpu.PrefetchScalarGridSpec(
            num_scalar_prefetch=1,
            grid=(rows // block,),
            in_specs=[tile(width), tile(width), whole((1, width)), whole((1, width)), whole((1, wide)), whole(merger.shape)]
            + [whole(part.shape) for part in parts],
            out_specs=[tile(width), tile(wide), tile(slim)],
            scratch_shapes=[pltpu.VMEM((width, wide), BF)],
        ),
        out_shape=[
            jax.ShapeDtypeStruct((rows, width), BF),
            jax.ShapeDtypeStruct((rows, wide), F32),
            jax.ShapeDtypeStruct((rows, slim), BF),
        ],
        cost_estimate=pl.CostEstimate(
            flops=2 * rows * width * (wide + slim), bytes_accessed=10 * rows * width, transcendentals=0
        ),
        compiler_params=pltpu.CompilerParams(vmem_limit_bytes=56 * 1024 * 1024),
    )(info, inputs, upstream, gain, shift, bias, merger, *parts)


def merge_kernel(m_ref, g_ref, f_ref, w_ref, out_ref, grad_ref):
    mixed = m_ref[...]
    out_ref[...] = (dot(mixed, w_ref[...], 1, 0) + f_ref[...].astype(F32)).astype(BF)
    add_to(grad_ref, pl.program_id(0), dot(mixed, g_ref[...], 0, 0))


def merge(mixed, upstream, partial, merger):
    rows, slim = mixed.shape
    width = upstream.shape[1]
    block = min(512, rows)

    def tile(n):
        return pl.BlockSpec((block, n), lambda i: (i, 0))

    return pl.pallas_call(
        merge_kernel,
        grid=(rows // block,),
        in_specs=[tile(slim), tile(width), tile(width), whole(merger.shape)],
        out_specs=[tile(width), whole((slim, width))],
        out_shape=[jax.ShapeDtypeStruct((rows, width), BF), jax.ShapeDtypeStruct((slim, width), F32)],
        cost_estimate=pl.CostEstimate(
            flops=4 * rows * width * slim, bytes_accessed=6 * rows * width, transcendentals=0
        ),
        compiler_params=pltpu.CompilerParams(vmem_limit_bytes=40 * 1024 * 1024),
    )(mixed, upstream, partial, merger)


def mixer_kernel(groups, info, x_ref, first_ref, e_ref, p_ref, gain_ref, *refs):
    parts = refs[:groups]
    out_ref, sums_ref, bsum_ref, s_ref, k_ref, mixer, total = refs[groups:]
    i = pl.program_id(0)
    group = info[0]
    share = mixer.shape[0] // groups

    @pl.when(i == 0)
    def _():
        lay(parts, mixer, group, share)

    grad = jnp.concatenate([p_ref[0], p_ref[1], p_ref[2]], 1)
    add_to(total, i, dot(first_ref[...], grad, 0, 0))
    first_grad = dot(grad, mixer[...], 1, 1)
    normed, _ = centre(x_ref[...].astype(F32))
    out_ref[...] = (first_grad * gain_ref[...] + e_ref[...].astype(F32)).astype(BF)
    add_rows(sums_ref, i, 0, first_grad * normed)
    add_rows(sums_ref, i, 1, first_grad)
    add_rows(bsum_ref, i, 0, grad.astype(F32))

    @pl.when(i == pl.num_programs(0) - 1)
    def _():
        split_out(total, s_ref, k_ref, group, share)


def mixer_back(info, inputs, first, error, grads, gain, parts):
    rows, width = inputs.shape
    groups = len(parts)
    wide = parts[0].shape[1]
    slim = wide // 3
    block = min(512, rows)
    shape = (groups // 2, width // groups, wide)
    tile = pl.BlockSpec((block, width), lambda i, _: (i, 0))
    return pl.pallas_call(
        functools.partial(mixer_kernel, groups),
        grid_spec=pltpu.PrefetchScalarGridSpec(
            num_scalar_prefetch=1,
            grid=(rows // block,),
            in_specs=[tile, tile, tile, pl.BlockSpec((3, block, slim), lambda i, _: (0, i, 0)), whole((1, width))]
            + [whole(part.shape) for part in parts],
            out_specs=[tile, whole((2, width)), whole((1, wide)), whole(shape), whole(shape)],
            scratch_shapes=[pltpu.VMEM((width, wide), BF), pltpu.VMEM((width, wide), F32)],
        ),
        out_shape=[
            jax.ShapeDtypeStruct((rows, width), BF),
            jax.ShapeDtypeStruct((2, width), F32),
            jax.ShapeDtypeStruct((1, wide), F32),
            jax.ShapeDtypeStruct(shape, BF),
            jax.ShapeDtypeStruct(shape, BF),
        ],
        cost_estimate=pl.CostEstimate(
            flops=4 * rows * width * wide, bytes_accessed=10 * rows * width, transcendentals=0
        ),
        compiler_params=pltpu.CompilerParams(vmem_limit_bytes=56 * 1024 * 1024),
    )(info, inputs, first, error, grads, gain, *parts)


def attend_kernel(heads, block, info, q_ref, k_ref, v_ref, g_ref, c_ref, s_ref, col_ref, row_ref, mixed_ref, grad_ref):
    length = q_ref.shape[0]
    half = ROT // 2
    cosine, sine = c_ref[0], s_ref[0]
    middle = length // 2
    low = pl.ds(pl.multiple_of(info[1] * middle, middle), middle)
    high = pl.ds(pl.multiple_of((1 - info[1]) * middle, middle), middle)

    def take(ref):
        return jnp.concatenate([ref[low, :], ref[high, :]], 0)

    def put(ref, value):
        ref[low, :] = value[:middle]
        ref[high, :] = value[middle:]

    def put_grad(part, value):
        grad_ref[part, low, :] = value[:middle]
        grad_ref[part, high, :] = value[middle:]

    lane = lax.broadcasted_iota(jnp.int32, cosine.shape, 1) % HD
    leading = lane < half

    def roll(value, shift):
        if value.shape[1] % 128:
            return jnp.concatenate([value[:, -shift:], value[:, :-shift]], 1)
        return pltpu.roll(value, shift % value.shape[1], 1)

    def turn(value):
        return value * cosine + jnp.where(leading, -roll(value, -half), roll(value, half)) * sine

    def turn_back(value):
        return value * cosine + jnp.where(leading, roll(value, -half), -roll(value, half)) * sine

    query = (turn(take(q_ref)).astype(BF).astype(F32) * SCALE).astype(BF)
    keys = turn(take(k_ref)).astype(BF)
    values = take(v_ref).astype(BF)
    grads = take(g_ref)
    col = col_ref[0]
    row = row_ref[0]
    dq_all, dk_all, dv_all, mixed_all = [], [], [], []
    for h in range(heads):
        span = slice(h * HD, (h + 1) * HD)
        qh, kh, vh, gh = query[:, span], keys[:, span], values[:, span], grads[:, span]
        dq_parts, mixed_parts = [], []
        dk = jnp.zeros((length, HD), F32)
        dv = jnp.zeros((length, HD), F32)
        for i in range(length // block):
            n = (i + 1) * block
            rows = slice(i * block, n)
            q, g = qh[rows], gh[rows]
            k, v = kh[:n], vh[:n]
            scores = dot(q, k, 1, 1)
            place_q = lax.broadcasted_iota(jnp.int32, (block, n), 0) + i * block
            place_k = lax.broadcasted_iota(jnp.int32, (block, n), 1)
            allowed = (col[rows] == row[:, :n]) & (place_q >= place_k)
            scores = jnp.where(allowed, scores, -1e30)
            expo = jnp.exp(scores - jnp.max(scores, -1, keepdims=True))
            prob = expo * (1.0 / jnp.sum(expo, -1, keepdims=True))
            prob_b = prob.astype(BF)
            mixed_parts.append(dot(prob_b, v, 1, 0))
            prob_grad = dot(g, v, 1, 1)
            center = jnp.sum(prob * prob_grad, -1, keepdims=True)
            score_grad = (prob * (prob_grad - center)).astype(BF)
            dq_parts.append(dot(score_grad, k, 1, 0) * SCALE)
            dk_add = dot(score_grad, q, 0, 0)
            dv_add = dot(prob_b, g, 0, 0)
            if n < length:
                zeros = jnp.zeros((length - n, HD), F32)
                dk_add = jnp.concatenate([dk_add, zeros], 0)
                dv_add = jnp.concatenate([dv_add, zeros], 0)
            dk = dk + dk_add
            dv = dv + dv_add
        dq_all.append(jnp.concatenate(dq_parts, 0))
        mixed_all.append(jnp.concatenate(mixed_parts, 0))
        dk_all.append(dk)
        dv_all.append(dv)
    put(mixed_ref, jnp.concatenate(mixed_all, 1).astype(BF))
    put_grad(0, turn_back(jnp.concatenate(dq_all, 1)).astype(BF))
    put_grad(1, turn_back(jnp.concatenate(dk_all, 1)).astype(BF))
    put_grad(2, jnp.concatenate(dv_all, 1).astype(BF))


def attend(info, project, mixed_grad, tables, segs):
    seqs, length = segs.shape
    rows, wide = project.shape
    width = wide // 3
    heads = min(2, width // HD)
    lanes = heads * HD
    steps = width // lanes
    block = min(256, length)

    parts = (project, project, project)
    ahead = steps
    if lanes % 128:
        parts = tuple(jnp.split(project, 3, 1))
        ahead = 0

    def of(part):
        return pl.BlockSpec((length, lanes), lambda s, h, _: (s, part * ahead + h))

    table = pl.BlockSpec((1, length, lanes), lambda s, h, _: (s, 0, 0))
    cost = pl.CostEstimate(
        flops=seqs * (width // HD) * length * length * HD * 12,
        bytes_accessed=rows * width * 24,
        transcendentals=seqs * (width // HD) * length * length,
    )
    return pl.pallas_call(
        functools.partial(attend_kernel, heads, block),
        grid_spec=pltpu.PrefetchScalarGridSpec(
            num_scalar_prefetch=1,
            grid=(seqs, steps),
            in_specs=[
                of(0),
                of(1),
                of(2),
                of(0),
                table,
                table,
                pl.BlockSpec((1, length, 1), lambda s, h, _: (s, 0, 0)),
                pl.BlockSpec((1, 1, length), lambda s, h, _: (s, 0, 0)),
            ],
            out_specs=[
                pl.BlockSpec((length, lanes), lambda s, h, _: (s, h)),
                pl.BlockSpec((3, length, lanes), lambda s, h, _: (0, s, h)),
            ],
        ),
        out_shape=[
            jax.ShapeDtypeStruct((rows, width), BF),
            jax.ShapeDtypeStruct((3, rows, width), BF),
        ],
        cost_estimate=cost,
        compiler_params=pltpu.CompilerParams(vmem_limit_bytes=56 * 1024 * 1024),
    )(info, *parts, mixed_grad, *tables, segs[:, :, None], segs[:, None, :])


def turn_tables(position, lanes):
    half = ROT // 2
    lane = jnp.arange(lanes) % HD
    freq = 10000.0 ** (-((lane % half).astype(F32) * 2.0) / float(ROT))
    freq = jnp.where(lane < ROT, freq, 0.0)
    phase = position.astype(F32)[..., None] * freq
    return jnp.cos(phase), jnp.sin(phase)


def local(
    tokens,
    segments,
    cotangent,
    mixer_gain,
    mixer_shift,
    mixer_weight,
    mixer_bias,
    merger_weight,
    merger_bias,
    feeder_gain,
    feeder_shift,
    widen_weight,
    widen_bias,
    narrow_weight,
    narrow_bias,
):
    seqs, stretch, width = tokens.shape
    seq = lax.axis_size("seq")
    groups = lax.axis_size("batch") // 2
    members = 2 * seq
    devices = groups * members
    length = stretch * seq
    here = lax.axis_index("seq")
    me = member()
    group = lax.axis_index("batch") // 2
    share = mixer_weight.shape[0]
    hidden = widen_weight.shape[1]
    slim = width // members
    unit = hidden // devices
    mine_h = groups * unit
    block = members * share
    turned = here if seq == 2 else jnp.zeros_like(here)
    info = jnp.stack([group, turned]).astype(jnp.int32)

    vectors = (mixer_gain, mixer_shift, mixer_bias, merger_bias, feeder_gain, feeder_shift, widen_bias, narrow_bias)
    sizes = [v.shape[0] for v in vectors]
    cuts = [sum(sizes[: i + 1]) for i in range(len(sizes) - 1)]
    packed = jnp.pad(jnp.concatenate(vectors), (0, mine_h - sum(sizes)))
    narrow_parts = gather_groups(narrow_weight)
    mixer_pieces = mixer_weight.reshape(share, 3, members, slim).transpose(2, 0, 1, 3)
    widen_pieces = widen_weight.reshape(share, groups, members, unit).transpose(2, 0, 1, 3)
    widen_pieces = jnp.concatenate(
        [
            widen_pieces.reshape(members, share, mine_h),
            jnp.broadcast_to(packed, (members, 1, mine_h)),
        ],
        1,
    )
    widen_got = exchange_members(widen_pieces)
    pad = (-members) % 16
    widen_chunk = jnp.concatenate(
        [widen_got[:, :share].reshape(block, mine_h), jnp.pad(widen_got[:, share], ((0, pad), (0, 0)))], 0
    )
    widen_parts = gather_groups(widen_chunk)
    mixer_chunk = exchange_members(mixer_pieces.reshape(members, share, 3 * slim)).reshape(block, -1)
    mixer_parts = gather_groups(after(mixer_chunk, widen_parts[-2]))
    merger = gather_merger(after(merger_weight, widen_parts[-2]))
    gathered = sort_groups(jnp.stack([p[block : block + members, : sum(sizes)] for p in widen_parts]))
    gathered = gathered.reshape(devices, -1).astype(F32)
    gain_m, shift_m, bias_m, bias_o, gain_f, shift_f, bias_w, bias_n = [
        v.reshape(1, -1) for v in jnp.split(gathered, cuts, 1)
    ]
    bias_m_mine = lax.dynamic_index_in_dim(bias_m.reshape(3, members, slim), me, 1).reshape(1, -1)
    bias_w_mine = lax.dynamic_index_in_dim(bias_w.reshape(groups, members, unit), me, 1).reshape(1, -1)

    inputs = join_tokens(tokens).reshape(-1, width)
    upstream = join_tokens(cotangent).reshape(-1, width)
    segs = join_tokens(segments)
    if seq == 2:
        flipped = jnp.concatenate([segs[:, stretch:], segs[:, :stretch]], 1)
        segs = jnp.where(here == 0, segs, flipped)
    place = jnp.arange(length, dtype=jnp.int32)
    earlier = jnp.sum((segs[:, None, :] < segs[:, :, None]).astype(jnp.int32), -1)
    tables = turn_tables(place[None, :] - earlier, min(2, slim // HD) * HD)

    partial, error, feed_sums, widen_bias_grad, n_send, n_keep, w_send, w_keep = feed(
        info, inputs, upstream, gain_f, shift_f, bias_w_mine, widen_parts, narrow_parts
    )
    narrow_out = reduce_groups(n_send, n_keep)
    widen_sum = reduce_groups(w_send, w_keep)
    widen_back = exchange_members(widen_sum.reshape(members, share, mine_h).astype(BF))
    widen_out = widen_back.reshape(members, share, groups, unit).transpose(1, 2, 0, 3).astype(F32)

    first, project, mixed_grad = project_all(
        info, inputs, after(upstream, partial), gain_m, shift_m, bias_m_mine, merger, mixer_parts
    )
    mixed, project_grad = attend(info, project, mixed_grad, tables, segs)
    partial, merger_grad = merge(mixed, upstream, partial, merger)
    merger_out = reduce_merger(merger_grad)
    own = tokens.astype(F32)
    layer_output = part_tokens(partial.reshape(2 * seqs, length, width))
    layer_output = (own + layer_output + (bias_o + bias_n)).astype(BF)
    error, mixer_sums, mixer_bias_grad, m_send, m_keep = mixer_back(
        info, inputs, first, error, project_grad, gain_m, mixer_parts
    )
    mixer_sum = reduce_groups(m_send, m_keep)
    mixer_back_rows = exchange_members(mixer_sum.reshape(members, share, 3 * slim).astype(BF))
    mixer_out = mixer_back_rows.reshape(members, share, 3, slim).transpose(1, 2, 0, 3).astype(F32)

    error = part_tokens(error.reshape(2 * seqs, length, width))
    normed, rstd = centre(own)
    back = rstd * (
        error
        - jnp.mean(error, -1, keepdims=True)
        - normed * jnp.mean(error * normed, -1, keepdims=True)
    )
    tokens_grad = (cotangent.astype(F32) + back).astype(BF)

    def spread_out(value, lead):
        shape = (lead, members, value.size // lead)
        return lax.dynamic_update_slice_in_dim(jnp.zeros(shape, F32), value.reshape(lead, 1, -1), me, 1)

    bias_grad = jnp.sum(cotangent.astype(F32), (0, 1))
    sums = (
        mixer_sums[0],
        mixer_sums[1],
        spread_out(mixer_bias_grad, 3),
        bias_grad,
        feed_sums[0],
        feed_sums[1],
        spread_out(widen_bias_grad, groups),
        bias_grad,
    )
    packed = jnp.concatenate([v.reshape(devices, -1) for v in sums], 1).reshape(groups, members, -1)
    relative = sort_groups(packed).reshape(groups // 2, 2, members, -1)
    owned = reduce_groups(relative[:, 1], relative[:, 0])
    owned = jnp.sum(exchange_members(owned), 0)
    gain_m_out, shift_m_out, bias_m_out, bias_o_out, gain_f_out, shift_f_out, bias_w_out, bias_n_out = jnp.split(owned, cuts)
    return (
        layer_output,
        tokens_grad,
        gain_m_out,
        shift_m_out,
        mixer_out.reshape(mixer_weight.shape),
        bias_m_out,
        merger_out,
        bias_o_out,
        gain_f_out,
        shift_f_out,
        widen_out.reshape(widen_weight.shape),
        bias_w_out,
        narrow_out,
        bias_n_out,
    )


def solution(mesh):
    vector = P(("batch", "seq"))
    matrix = P(("batch", "seq"), None)
    rows = P("batch", "seq", None)
    params = (vector, vector, matrix, vector, matrix, vector, vector, vector, matrix, vector, matrix, vector)
    return jax.shard_map(
        local,
        mesh=mesh,
        in_specs=(rows, P("batch", "seq"), rows) + params,
        out_specs=(rows, rows) + params,
        check_vma=False,
    )
```

```python
import functools

import jax
import jax.numpy as jnp
from jax import lax
from jax.experimental import pallas as pl
from jax.experimental.pallas import tpu as pltpu
from jax.sharding import PartitionSpec as P

HD = 64
ROT = 16
EPS = 1e-05
SCALE = 0.125
F32 = jnp.float32
BF = jnp.bfloat16


def dot(left, right, left_dim, right_dim):
    return lax.dot_general(
        left, right, (((left_dim,), (right_dim,)), ((), ())), preferred_element_type=F32
    )


def swap_batch(value, mask):
    count = lax.axis_size("batch")
    return lax.ppermute(value, "batch", [(i, i ^ mask) for i in range(count)])


def swap_seq(value, mask):
    count = lax.axis_size("seq")
    return lax.ppermute(value, "seq", [(i, i ^ mask) for i in range(count)])


def swap_member(value, mask):
    members = 2 * lax.axis_size("seq")
    count = lax.axis_size("batch") * lax.axis_size("seq")
    return lax.ppermute(
        value,
        ("batch", "seq"),
        [(i, (i // members) * members + ((i % members) ^ mask)) for i in range(count)],
    )


def after(value, *others):
    return lax.optimization_barrier((value,) + others)[0]


def sort_groups(value):
    groups = value.shape[0]
    me = lax.axis_index("batch") // 2
    bit = 1
    while bit < groups:
        paired = value.reshape((groups // (2 * bit), 2, bit) + value.shape[1:])
        flipped = jnp.concatenate([paired[:, 1:], paired[:, :1]], 1)
        value = jnp.where((me & bit) > 0, flipped, paired).reshape(value.shape)
        bit = 2 * bit
    return value


LIGHT = pl.CostEstimate(flops=1000, bytes_accessed=1000, transcendentals=0)


def far_groups(chunk):
    groups = lax.axis_size("batch") // 2
    return jnp.stack([chunk] + [swap_batch(chunk, 4 * k) for k in range(1, groups // 2)])


def near_groups(stack):
    return swap_batch(stack, 2)


def fold_near(send, keep):
    return send.shape[0], keep, swap_batch(send, 2), send.dtype


def fold_far(state, *others):
    half, keep, got, dtype = state
    total = keep[0].astype(F32) + got[0].astype(F32)
    for k in range(1, half):
        piece = (keep[k].astype(F32) + got[k].astype(F32)).astype(dtype)
        total = total + swap_batch(after(piece, *others), 4 * k).astype(F32)
    return total


def member():
    return (lax.axis_index("batch") % 2) * lax.axis_size("seq") + lax.axis_index("seq")


def exchange_members(pieces):
    me = member()
    out = jnp.zeros_like(pieces)
    for k in range(pieces.shape[0]):
        piece = lax.dynamic_index_in_dim(pieces, me ^ k, 0, keepdims=True)
        got = piece if k == 0 else swap_member(piece, k)
        out = lax.dynamic_update_slice_in_dim(out, got, me ^ k, 0)
    return out


def gather_merger(block):
    seq = lax.axis_size("seq")
    batch = lax.axis_size("batch")
    members = 2 * seq
    groups = batch // 2
    lows = groups // members
    every = ("batch", "seq")
    group = lax.axis_index("batch") // 2
    root = group // lows
    found = jnp.where(member() == root, block, jnp.zeros_like(block))
    for k in range(1, members):
        pairs = [
            (g * members + g // lows, (g ^ (k * lows)) * members + g // lows) for g in range(groups)
        ]
        found = found + lax.ppermute(block, every, pairs)
    whole = found[None]
    bit = 1
    while bit < lows:
        got = swap_batch(whole, 2 * bit)
        swapped = (group & bit) > 0
        whole = jnp.where(swapped, jnp.concatenate([got, whole]), jnp.concatenate([whole, got]))
        bit = 2 * bit
    return whole.reshape(-1, block.shape[1])


def far_tokens(value, *others):
    if lax.axis_size("seq") == 2:
        return jnp.concatenate([value, swap_seq(after(value, *others), 1)], 1)
    return lax.all_gather(value, "seq", axis=1, tiled=True)


def near_tokens(value, *others):
    seqs = value.shape[0] // 2
    return value[:seqs].astype(F32) + swap_batch(value[seqs:], 1).astype(F32)


def part_tokens(mine, *others):
    if lax.axis_size("seq") == 2:
        stretch = mine.shape[1] // 2
        return mine[:, :stretch] + swap_seq(after(mine[:, stretch:].astype(BF), *others), 1).astype(F32)
    return lax.psum_scatter(mine.astype(BF), "seq", scatter_dimension=1, tiled=True).astype(F32)


def reduce_merger(grad):
    seq = lax.axis_size("seq")
    batch = lax.axis_size("batch")
    members = 2 * seq
    groups = batch // 2
    lows = groups // members
    every = ("batch", "seq")
    group = lax.axis_index("batch") // 2
    root = group // lows
    me = member()
    whole = grad.reshape((lows, -1, grad.shape[1]))
    bit = lows // 2
    while bit:
        halves = whole.reshape((2, -1) + whole.shape[1:])
        side = ((group & bit) > 0).astype(jnp.int32)
        away = lax.dynamic_index_in_dim(halves, 1 - side, 0, keepdims=False).astype(BF)
        whole = lax.dynamic_index_in_dim(halves, side, 0, keepdims=False)
        whole = whole + swap_batch(away, 2 * bit).astype(F32)
        bit = bit // 2
    block = whole[0].astype(BF)
    total = whole[0]
    for k in range(1, members):
        pairs = [
            ((g ^ (k * lows)) * members + g // lows, g * members + g // lows) for g in range(groups)
        ]
        total = total + lax.ppermute(block, every, pairs).astype(F32)
    rows = total.reshape(members, -1, grad.shape[1]).astype(BF)
    mine = lax.dynamic_index_in_dim(rows, me, 0, keepdims=False).astype(F32)
    out = jnp.where(me == root, mine, jnp.zeros_like(mine))
    for k in range(1, members):
        pairs = [
            (g * members + g // lows, g * members + ((g // lows) ^ k)) for g in range(groups)
        ]
        piece = lax.dynamic_index_in_dim(rows, me ^ k, 0, keepdims=False)
        out = out + lax.ppermute(piece, every, pairs).astype(F32)
    return out


def centre(rows):
    mean = jnp.mean(rows, -1, keepdims=True)
    centered = rows - mean
    spread = jnp.mean(centered * centered, -1, keepdims=True)
    rstd = lax.rsqrt(spread + EPS)
    return centered * rstd, rstd


def lay(far, near, out_ref, group, rows):
    for k in range(far.shape[0]):
        out_ref[pl.ds(pl.multiple_of((group ^ (2 * k)) * rows, rows), rows), :] = far[k, :rows, :]
        out_ref[pl.ds(pl.multiple_of((group ^ (2 * k + 1)) * rows, rows), rows), :] = near[k, :rows, :]


def pick(own, peer):
    return jnp.where(pl.program_id(0) < pl.num_programs(0) // 2, own[...], peer[...])


def split_out(total_ref, send_ref, keep_ref, group, rows):
    for k in range(send_ref.shape[0]):
        keep = pl.multiple_of((group ^ (2 * k)) * rows, rows)
        send = pl.multiple_of((group ^ (2 * k + 1)) * rows, rows)
        keep_ref[k] = total_ref[pl.ds(keep, rows), :].astype(BF)
        send_ref[k] = total_ref[pl.ds(send, rows), :].astype(BF)


def add_rows(out_ref, i, row, value):
    total = jnp.sum(value, 0, keepdims=True)

    @pl.when(i == 0)
    def _():
        out_ref[row : row + 1, :] = total

    @pl.when(i > 0)
    def _():
        out_ref[row : row + 1, :] += total


def add_to(total_ref, i, value):
    @pl.when(i == 0)
    def _():
        total_ref[...] = value

    @pl.when(i > 0)
    def _():
        total_ref[...] += value


def whole(shape):
    return pl.BlockSpec(shape, lambda *_: (0,) * len(shape), pipeline_mode=pl.Buffered(1))


def widen_kernel(info, xo_ref, xp_ref, go_ref, gp_ref, gain_ref, shift_ref, bias_ref, far_ref, near_ref, *refs):
    active_ref, slope_ref, send_ref, keep_ref, widen, total = refs
    i = pl.program_id(0)
    group = info[0]
    share = widen.shape[0] // (2 * far_ref.shape[0])

    @pl.when(i == 0)
    def _():
        lay(far_ref, near_ref, widen, group, share)

    normed, _ = centre(pick(xo_ref, xp_ref).astype(F32))
    second = (normed * gain_ref[...] + shift_ref[...]).astype(BF)
    widened = dot(second, widen[...], 1, 0) + bias_ref[...]
    bell = 0.5 + 0.5 * lax.erf(widened * (0.5**0.5))
    active = (widened * bell).astype(BF)
    slope = bell + widened * jnp.exp(-0.5 * widened * widened) * (0.15915494309189535**0.5)
    active_ref[...] = active
    slope_ref[...] = slope.astype(BF)
    add_to(total, i, dot(active, pick(go_ref, gp_ref), 0, 0))

    @pl.when(i == pl.num_programs(0) - 1)
    def _():
        split_out(total, send_ref, keep_ref, group, total.shape[0] // (2 * far_ref.shape[0]))


def narrow_kernel(info, xo_ref, xp_ref, go_ref, gp_ref, a_ref, s_ref, gain_ref, shift_ref, *refs):
    wf_ref, wn_ref, nf_ref, nn_ref, out_ref, e_ref, sums_ref, bsum_ref, send_ref, keep_ref, widen, narrow, total = refs
    i = pl.program_id(0)
    group = info[0]
    groups = 2 * wf_ref.shape[0]
    share = widen.shape[0] // groups

    @pl.when(i == 0)
    def _():
        lay(wf_ref, wn_ref, widen, group, share)
        lay(nf_ref, nn_ref, narrow, group, narrow.shape[0] // groups)

    out_ref[...] = dot(a_ref[...], narrow[...], 1, 0).astype(BF)
    active_grad = dot(pick(go_ref, gp_ref), narrow[...], 1, 1)
    widened_grad = (active_grad * s_ref[...].astype(F32)).astype(BF)
    add_rows(bsum_ref, i, 0, widened_grad.astype(F32))
    normed, _ = centre(pick(xo_ref, xp_ref).astype(F32))
    second = (normed * gain_ref[...] + shift_ref[...]).astype(BF)
    add_to(total, i, dot(second, widened_grad, 0, 0))
    second_grad = dot(widened_grad, widen[...], 1, 1)
    add_rows(sums_ref, i, 0, second_grad * normed)
    add_rows(sums_ref, i, 1, second_grad)
    e_ref[...] = (second_grad * gain_ref[...]).astype(BF)

    @pl.when(i == pl.num_programs(0) - 1)
    def _():
        split_out(total, send_ref, keep_ref, group, share)


def tiles(rows):
    block = min(512, rows)
    steps = 2 * rows // block

    def own(n):
        return pl.BlockSpec((block, n), lambda i, *_: (jnp.minimum(i, steps // 2 - 1), 0))

    def peer(n):
        return pl.BlockSpec((block, n), lambda i, *_: (jnp.maximum(i - steps // 2, 0), 0))

    def every(n):
        return pl.BlockSpec((block, n), lambda i, *_: (i, 0))

    return block, steps, own, peer, every


def call(kernel, steps, in_specs, out_specs, out_shape, scratch, *operands):
    return pl.pallas_call(
        kernel,
        grid_spec=pltpu.PrefetchScalarGridSpec(
            num_scalar_prefetch=1, grid=(steps,), in_specs=in_specs, out_specs=out_specs, scratch_shapes=scratch
        ),
        out_shape=out_shape,
        cost_estimate=LIGHT,
        compiler_params=pltpu.CompilerParams(vmem_limit_bytes=58 * 1024 * 1024),
    )(*operands)


def feed_widen(info, inputs, upstream, gain, shift, bias, far, near):
    rows, width = inputs[0].shape
    half, _, hidden = far.shape
    _, steps, own, peer, every = tiles(rows)
    shape = (half, hidden // (2 * half), width)
    return call(
        widen_kernel,
        steps,
        [own(width), peer(width), own(width), peer(width), whole((1, width)), whole((1, width)), whole((1, hidden))]
        + [whole(far.shape), whole(near.shape)],
        [every(hidden), every(hidden), whole(shape), whole(shape)],
        [jax.ShapeDtypeStruct((2 * rows, hidden), BF)] * 2 + [jax.ShapeDtypeStruct(shape, BF)] * 2,
        [pltpu.VMEM((width, hidden), BF), pltpu.VMEM((hidden, width), F32)],
        info, *inputs, *upstream, gain, shift, bias, far, near,
    )


def feed_narrow(info, inputs, upstream, active, slope, gain, shift, widen, narrow):
    rows, width = inputs[0].shape
    half, _, hidden = widen[0].shape
    _, steps, own, peer, every = tiles(rows)
    shape = (half, width // (2 * half), hidden)
    return call(
        narrow_kernel,
        steps,
        [own(width), peer(width), own(width), peer(width), every(hidden), every(hidden), whole((1, width)), whole((1, width))]
        + [whole(part.shape) for part in widen + narrow],
        [every(width), every(width), whole((2, width)), whole((1, hidden)), whole(shape), whole(shape)],
        [
            jax.ShapeDtypeStruct((2 * rows, width), BF),
            jax.ShapeDtypeStruct((2 * rows, width), BF),
            jax.ShapeDtypeStruct((2, width), F32),
            jax.ShapeDtypeStruct((1, hidden), F32),
            jax.ShapeDtypeStruct(shape, BF),
            jax.ShapeDtypeStruct(shape, BF),
        ],
        [pltpu.VMEM((width, hidden), BF), pltpu.VMEM((hidden, width), BF), pltpu.VMEM((width, hidden), F32)],
        info, *inputs, *upstream, active, slope, gain, shift, *widen, *narrow,
    )


def project_kernel(info, xo_ref, xp_ref, go_ref, gp_ref, gain_ref, shift_ref, bias_ref, merger_ref, far_ref, near_ref, *refs):
    first_ref, project_ref, mg_ref, mixer = refs

    @pl.when(pl.program_id(0) == 0)
    def _():
        lay(far_ref, near_ref, mixer, info[0], mixer.shape[0] // (2 * far_ref.shape[0]))

    normed, _ = centre(pick(xo_ref, xp_ref).astype(F32))
    first = (normed * gain_ref[...] + shift_ref[...]).astype(BF)
    first_ref[...] = first
    project_ref[...] = dot(first, mixer[...], 1, 0) + bias_ref[...]
    mg_ref[...] = dot(pick(go_ref, gp_ref), merger_ref[...], 1, 1).astype(BF)


def project_all(info, inputs, upstream, gain, shift, bias, merger, far, near):
    rows, width = inputs[0].shape
    wide = far.shape[2]
    slim = wide // 3
    _, steps, own, peer, every = tiles(rows)
    return call(
        project_kernel,
        steps,
        [own(width), peer(width), own(width), peer(width), whole((1, width)), whole((1, width)), whole((1, wide))]
        + [whole(merger.shape), whole(far.shape), whole(near.shape)],
        [every(width), every(wide), every(slim)],
        [
            jax.ShapeDtypeStruct((2 * rows, width), BF),
            jax.ShapeDtypeStruct((2 * rows, wide), F32),
            jax.ShapeDtypeStruct((2 * rows, slim), BF),
        ],
        [pltpu.VMEM((width, wide), BF)],
        info, *inputs, *upstream, gain, shift, bias, merger, far, near,
    )


def merge_kernel(info, m_ref, go_ref, gp_ref, f_ref, w_ref, out_ref, grad_ref):
    mixed = m_ref[...]
    out_ref[...] = (dot(mixed, w_ref[...], 1, 0) + f_ref[...].astype(F32)).astype(BF)
    add_to(grad_ref, pl.program_id(0), dot(mixed, pick(go_ref, gp_ref), 0, 0))


def merge(info, mixed, upstream, partial, merger):
    rows, width = upstream[0].shape
    slim = mixed.shape[1]
    _, steps, own, peer, every = tiles(rows)
    return call(
        merge_kernel,
        steps,
        [every(slim), own(width), peer(width), every(width), whole(merger.shape)],
        [every(width), whole((slim, width))],
        [jax.ShapeDtypeStruct((2 * rows, width), BF), jax.ShapeDtypeStruct((slim, width), F32)],
        [],
        info, mixed, *upstream, partial, merger,
    )


def mixer_kernel(info, xo_ref, xp_ref, first_ref, e_ref, p_ref, gain_ref, far_ref, near_ref, *refs):
    out_ref, sums_ref, bsum_ref, send_ref, keep_ref, mixer, total = refs
    i = pl.program_id(0)
    group = info[0]
    share = mixer.shape[0] // (2 * far_ref.shape[0])

    @pl.when(i == 0)
    def _():
        lay(far_ref, near_ref, mixer, group, share)

    grad = jnp.concatenate([p_ref[0], p_ref[1], p_ref[2]], 1)
    add_to(total, i, dot(first_ref[...], grad, 0, 0))
    first_grad = dot(grad, mixer[...], 1, 1)
    normed, _ = centre(pick(xo_ref, xp_ref).astype(F32))
    out_ref[...] = (first_grad * gain_ref[...] + e_ref[...].astype(F32)).astype(BF)
    add_rows(sums_ref, i, 0, first_grad * normed)
    add_rows(sums_ref, i, 1, first_grad)
    add_rows(bsum_ref, i, 0, grad.astype(F32))

    @pl.when(i == pl.num_programs(0) - 1)
    def _():
        split_out(total, send_ref, keep_ref, group, share)


def mixer_back(info, inputs, first, error, grads, gain, far, near):
    rows, width = inputs[0].shape
    half, _, wide = far.shape
    block, steps, own, peer, every = tiles(rows)
    shape = (half, width // (2 * half), wide)
    return call(
        mixer_kernel,
        steps,
        [own(width), peer(width), every(width), every(width)]
        + [pl.BlockSpec((3, block, wide // 3), lambda i, _: (0, i, 0)), whole((1, width))]
        + [whole(far.shape), whole(near.shape)],
        [every(width), whole((2, width)), whole((1, wide)), whole(shape), whole(shape)],
        [
            jax.ShapeDtypeStruct((2 * rows, width), BF),
            jax.ShapeDtypeStruct((2, width), F32),
            jax.ShapeDtypeStruct((1, wide), F32),
            jax.ShapeDtypeStruct(shape, BF),
            jax.ShapeDtypeStruct(shape, BF),
        ],
        [pltpu.VMEM((width, wide), BF), pltpu.VMEM((width, wide), F32)],
        info, *inputs, first, error, grads, gain, far, near,
    )


def attend_kernel(heads, block, info, q_ref, k_ref, v_ref, g_ref, c_ref, s_ref, col_ref, row_ref, mixed_ref, grad_ref):
    length = q_ref.shape[0]
    half = ROT // 2
    cosine, sine = c_ref[0], s_ref[0]
    middle = length // 2
    low = pl.ds(pl.multiple_of(info[1] * middle, middle), middle)
    high = pl.ds(pl.multiple_of((1 - info[1]) * middle, middle), middle)

    def take(ref):
        return jnp.concatenate([ref[low, :], ref[high, :]], 0)

    def put(ref, value):
        ref[low, :] = value[:middle]
        ref[high, :] = value[middle:]

    def put_grad(part, value):
        grad_ref[part, low, :] = value[:middle]
        grad_ref[part, high, :] = value[middle:]

    lane = lax.broadcasted_iota(jnp.int32, cosine.shape, 1) % HD
    leading = lane < half

    def roll(value, shift):
        if value.shape[1] % 128:
            return jnp.concatenate([value[:, -shift:], value[:, :-shift]], 1)
        return pltpu.roll(value, shift % value.shape[1], 1)

    def turn(value):
        return value * cosine + jnp.where(leading, -roll(value, -half), roll(value, half)) * sine

    def turn_back(value):
        return value * cosine + jnp.where(leading, roll(value, -half), -roll(value, half)) * sine

    query = (turn(take(q_ref)).astype(BF).astype(F32) * SCALE).astype(BF)
    keys = turn(take(k_ref)).astype(BF)
    values = take(v_ref).astype(BF)
    grads = take(g_ref)
    col = col_ref[0]
    row = row_ref[0]
    dq_all, dk_all, dv_all, mixed_all = [], [], [], []
    for h in range(heads):
        span = slice(h * HD, (h + 1) * HD)
        qh, kh, vh, gh = query[:, span], keys[:, span], values[:, span], grads[:, span]
        dq_parts, mixed_parts = [], []
        dk = jnp.zeros((length, HD), F32)
        dv = jnp.zeros((length, HD), F32)
        for i in range(length // block):
            n = (i + 1) * block
            rows = slice(i * block, n)
            q, g = qh[rows], gh[rows]
            k, v = kh[:n], vh[:n]
            scores = dot(q, k, 1, 1)
            place_q = lax.broadcasted_iota(jnp.int32, (block, n), 0) + i * block
            place_k = lax.broadcasted_iota(jnp.int32, (block, n), 1)
            allowed = (col[rows] == row[:, :n]) & (place_q >= place_k)
            scores = jnp.where(allowed, scores, -1e30)
            expo = jnp.exp(scores - jnp.max(scores, -1, keepdims=True))
            prob = expo * (1.0 / jnp.sum(expo, -1, keepdims=True))
            prob_b = prob.astype(BF)
            mixed_parts.append(dot(prob_b, v, 1, 0))
            prob_grad = dot(g, v, 1, 1)
            center = jnp.sum(prob * prob_grad, -1, keepdims=True)
            score_grad = (prob * (prob_grad - center)).astype(BF)
            dq_parts.append(dot(score_grad, k, 1, 0) * SCALE)
            dk_add = dot(score_grad, q, 0, 0)
            dv_add = dot(prob_b, g, 0, 0)
            if n < length:
                zeros = jnp.zeros((length - n, HD), F32)
                dk_add = jnp.concatenate([dk_add, zeros], 0)
                dv_add = jnp.concatenate([dv_add, zeros], 0)
            dk = dk + dk_add
            dv = dv + dv_add
        dq_all.append(jnp.concatenate(dq_parts, 0))
        mixed_all.append(jnp.concatenate(mixed_parts, 0))
        dk_all.append(dk)
        dv_all.append(dv)
    put(mixed_ref, jnp.concatenate(mixed_all, 1).astype(BF))
    put_grad(0, turn_back(jnp.concatenate(dq_all, 1)).astype(BF))
    put_grad(1, turn_back(jnp.concatenate(dk_all, 1)).astype(BF))
    put_grad(2, jnp.concatenate(dv_all, 1).astype(BF))


def attend(info, side, project, mixed_grad, tables, segs):
    seqs, length = segs.shape
    seqs = seqs // 2
    skip = side * seqs
    wide = project.shape[1]
    rows = seqs * length
    width = wide // 3
    heads = min(2, width // HD)
    lanes = heads * HD
    steps = width // lanes
    block = min(256, length)

    parts = (project, project, project)
    ahead = steps
    if lanes % 128:
        parts = tuple(jnp.split(project, 3, 1))
        ahead = 0

    def of(part):
        return pl.BlockSpec((length, lanes), lambda s, h, _: (s + skip, part * ahead + h))

    table = pl.BlockSpec((1, length, lanes), lambda s, h, _: (s + skip, 0, 0))
    return pl.pallas_call(
        functools.partial(attend_kernel, heads, block),
        grid_spec=pltpu.PrefetchScalarGridSpec(
            num_scalar_prefetch=1,
            grid=(seqs, steps),
            in_specs=[
                of(0),
                of(1),
                of(2),
                of(0),
                table,
                table,
                pl.BlockSpec((1, length, 1), lambda s, h, _: (s + skip, 0, 0)),
                pl.BlockSpec((1, 1, length), lambda s, h, _: (s + skip, 0, 0)),
            ],
            out_specs=[
                pl.BlockSpec((length, lanes), lambda s, h, _: (s, h)),
                pl.BlockSpec((3, length, lanes), lambda s, h, _: (0, s, h)),
            ],
        ),
        out_shape=[
            jax.ShapeDtypeStruct((rows, width), BF),
            jax.ShapeDtypeStruct((3, rows, width), BF),
        ],
        cost_estimate=LIGHT,
        compiler_params=pltpu.CompilerParams(vmem_limit_bytes=56 * 1024 * 1024),
    )(info, *parts, mixed_grad, *tables, segs[:, :, None], segs[:, None, :])


def turn_tables(position, lanes):
    half = ROT // 2
    lane = jnp.arange(lanes) % HD
    freq = 10000.0 ** (-((lane % half).astype(F32) * 2.0) / float(ROT))
    freq = jnp.where(lane < ROT, freq, 0.0)
    phase = position.astype(F32)[..., None] * freq
    return jnp.cos(phase), jnp.sin(phase)


def local(
    tokens,
    segments,
    cotangent,
    mixer_gain,
    mixer_shift,
    mixer_weight,
    mixer_bias,
    merger_weight,
    merger_bias,
    feeder_gain,
    feeder_shift,
    widen_weight,
    widen_bias,
    narrow_weight,
    narrow_bias,
):
    seqs, stretch, width = tokens.shape
    seq = lax.axis_size("seq")
    groups = lax.axis_size("batch") // 2
    members = 2 * seq
    devices = groups * members
    length = stretch * seq
    here = lax.axis_index("seq")
    me = member()
    group = lax.axis_index("batch") // 2
    share = mixer_weight.shape[0]
    hidden = widen_weight.shape[1]
    slim = width // members
    unit = hidden // devices
    mine_h = groups * unit
    block = members * share
    wide = 3 * slim
    turned = here if seq == 2 else jnp.zeros_like(here)
    info = jnp.stack([group, turned]).astype(jnp.int32)

    vectors = (mixer_gain, mixer_shift, mixer_bias, merger_bias, feeder_gain, feeder_shift, widen_bias, narrow_bias)
    sizes = [v.shape[0] for v in vectors]
    cuts = [sum(sizes[: i + 1]) for i in range(len(sizes) - 1)]
    span = wide + mine_h + width
    packed = jnp.concatenate(vectors)
    small = jnp.stack(
        [
            jnp.pad(packed, (0, span - packed.size)),
            jnp.pad(segments.reshape(-1).astype(BF), (0, span - segments.size)),
        ]
    )
    mixer_pieces = mixer_weight.reshape(share, 3, members, slim).transpose(2, 0, 1, 3)
    widen_pieces = widen_weight.reshape(share, groups, members, unit).transpose(2, 0, 1, 3)
    pieces = jnp.concatenate(
        [
            jnp.concatenate(
                [
                    mixer_pieces.reshape(members, share, wide),
                    widen_pieces.reshape(members, share, mine_h),
                    jnp.broadcast_to(merger_weight, (members, share, width)),
                ],
                2,
            ),
            jnp.broadcast_to(small, (members, 2, span)),
        ],
        1,
    )
    got = exchange_members(pieces)
    pad = (-members) % 16
    notes = jnp.pad(got[:, share, : sum(sizes)], ((0, pad), (0, 0)))
    columns = max(wide, sum(sizes))
    notes = jnp.pad(notes, ((0, 0), (0, columns - sum(sizes))))
    mixer_chunk = got[:, :share, :wide].reshape(block, wide)
    widen_chunk = got[:, :share, wide : wide + mine_h].reshape(block, mine_h)
    merger_block = got[:, :share, wide + mine_h :].reshape(block, width)
    segs = got[:, share + 1, : segments.size].astype(jnp.int32).reshape(2, seq, seqs, stretch)
    segs = segs.transpose(0, 2, 1, 3).reshape(2, seqs, length)
    segs = jnp.where(lax.axis_index("batch") % 2 == 0, segs, segs[::-1]).reshape(2 * seqs, length)

    mixer_far = far_groups(jnp.concatenate([mixer_chunk, notes[:, :wide]], 0))
    inputs_own = far_tokens(tokens, got).reshape(-1, width)
    merger = gather_merger(merger_block)
    mixer_near = near_groups(mixer_far)
    widen_far = far_groups(after(widen_chunk, mixer_far))
    inputs = (inputs_own, swap_batch(inputs_own, 1))
    upstream_own = far_tokens(cotangent, inputs_own).reshape(-1, width)
    upstream = (upstream_own, swap_batch(upstream_own, 1))
    widen_near = near_groups(after(widen_far, mixer_near))
    narrow_far = far_groups(after(narrow_weight, widen_far))
    narrow_near = near_groups(after(narrow_far, widen_near))
    widen = (widen_far, widen_near)
    narrow = (narrow_far, narrow_near)

    both = jnp.stack([mixer_far[:, block : block + members], mixer_near[:, block : block + members]], 1)
    gathered = sort_groups(both.reshape(groups, members, -1)[:, :, : sum(sizes)])
    gathered = gathered.reshape(devices, -1).astype(F32)
    gain_m, shift_m, bias_m, bias_o, gain_f, shift_f, bias_w, bias_n = [
        v.reshape(1, -1) for v in jnp.split(gathered, cuts, 1)
    ]
    bias_m_mine = lax.dynamic_index_in_dim(bias_m.reshape(3, members, slim), me, 1).reshape(1, -1)
    bias_w_mine = lax.dynamic_index_in_dim(bias_w.reshape(groups, members, unit), me, 1).reshape(1, -1)
    place = jnp.arange(length, dtype=jnp.int32)
    earlier = jnp.sum((segs[:, None, :] < segs[:, :, None]).astype(jnp.int32), -1)
    tables = turn_tables(place[None, :] - earlier, min(2, slim // HD) * HD)

    first, project, mixed_grad = project_all(
        info, inputs, upstream, gain_m, shift_m, bias_m_mine, merger, mixer_far, mixer_near
    )
    mixed_a, grad_a = attend(info, 0, project, mixed_grad, tables, segs)

    active, slope, n_send, n_keep = feed_widen(
        after(info, mixed_a, narrow_far), inputs, upstream, gain_f, shift_f, bias_w_mine, widen_far, widen_near
    )
    narrow_state = fold_near(n_send, n_keep)

    mixed_b, grad_b = attend(after(info, active), 1, project, mixed_grad, tables, segs)

    partial, error, feed_sums, widen_bias_grad, w_send, w_keep = feed_narrow(
        after(info, mixed_b, narrow_state[2]), inputs, upstream, active, slope, gain_f, shift_f, widen, narrow
    )
    narrow_out = fold_far(narrow_state)
    widen_state = fold_near(after(w_send, narrow_state[2]), w_keep)

    mixed = jnp.concatenate([mixed_a, mixed_b], 0)
    project_grad = jnp.concatenate([grad_a, grad_b], 1)
    partial, merger_grad = merge(info, mixed, upstream, partial, merger)
    error, mixer_sums, mixer_bias_grad, m_send, m_keep = mixer_back(
        after(info, partial), inputs, first, error, project_grad, gain_m, mixer_far, mixer_near
    )
    own = tokens.astype(F32)
    layer_output = part_tokens(near_tokens(partial.reshape(2 * seqs, length, width)))
    mixer_state = fold_near(after(m_send, widen_state[2]), m_keep)
    widen_sum = fold_far(widen_state, narrow_out)
    merger_out = reduce_merger(merger_grad)
    widen_back = exchange_members(widen_sum.reshape(members, share, mine_h).astype(BF))
    widen_out = widen_back.reshape(members, share, groups, unit).transpose(1, 2, 0, 3).astype(F32)
    mixer_sum = fold_far(mixer_state, widen_sum)
    mixer_back_rows = exchange_members(mixer_sum.reshape(members, share, wide).astype(BF))
    mixer_out = mixer_back_rows.reshape(members, share, 3, slim).transpose(1, 2, 0, 3).astype(F32)

    error = part_tokens(near_tokens(error.reshape(2 * seqs, length, width)), layer_output)
    layer_output = (own + layer_output + (bias_o + bias_n)).astype(BF)
    normed, rstd = centre(own)
    back = rstd * (
        error
        - jnp.mean(error, -1, keepdims=True)
        - normed * jnp.mean(error * normed, -1, keepdims=True)
    )
    tokens_grad = (cotangent.astype(F32) + back).astype(BF)

    def spread_out(value, lead):
        shape = (lead, members, value.size // lead)
        return lax.dynamic_update_slice_in_dim(jnp.zeros(shape, F32), value.reshape(lead, 1, -1), me, 1)

    bias_grad = jnp.sum(cotangent.astype(F32), (0, 1))
    sums = (
        mixer_sums[0],
        mixer_sums[1],
        spread_out(mixer_bias_grad, 3),
        bias_grad,
        feed_sums[0],
        feed_sums[1],
        spread_out(widen_bias_grad, groups),
        bias_grad,
    )
    packed = jnp.concatenate([v.reshape(devices, -1) for v in sums], 1).reshape(groups, members, -1)
    relative = sort_groups(packed).reshape(groups // 2, 2, members, -1)
    owned = fold_far(fold_near(relative[:, 1], relative[:, 0]))
    owned = jnp.sum(exchange_members(owned), 0)
    gain_m_out, shift_m_out, bias_m_out, bias_o_out, gain_f_out, shift_f_out, bias_w_out, bias_n_out = jnp.split(owned, cuts)
    return (
        layer_output,
        tokens_grad,
        gain_m_out,
        shift_m_out,
        mixer_out.reshape(mixer_weight.shape),
        bias_m_out,
        merger_out,
        bias_o_out,
        gain_f_out,
        shift_f_out,
        widen_out.reshape(widen_weight.shape),
        bias_w_out,
        narrow_out,
        bias_n_out,
    )


def solution(mesh):
    vector = P(("batch", "seq"))
    matrix = P(("batch", "seq"), None)
    rows = P("batch", "seq", None)
    params = (vector, vector, matrix, vector, matrix, vector, vector, vector, matrix, vector, matrix, vector)
    return jax.shard_map(
        local,
        mesh=mesh,
        in_specs=(rows, P("batch", "seq"), rows) + params,
        out_specs=(rows, rows) + params,
        check_vma=False,
    )
```

```python
import functools

import jax
import jax.numpy as jnp
from jax import lax
from jax.experimental import pallas as pl
from jax.experimental.pallas import tpu as pltpu
from jax.sharding import PartitionSpec as P

HD = 64
ROT = 16
EPS = 1e-05
SCALE = 0.125
F32 = jnp.float32
BF = jnp.bfloat16


def dot(left, right, left_dim, right_dim):
    return lax.dot_general(
        left, right, (((left_dim,), (right_dim,)), ((), ())), preferred_element_type=F32
    )


def swap_batch(value, mask):
    count = lax.axis_size("batch")
    return lax.ppermute(value, "batch", [(i, i ^ mask) for i in range(count)])


def swap_seq(value, mask):
    count = lax.axis_size("seq")
    return lax.ppermute(value, "seq", [(i, i ^ mask) for i in range(count)])


def swap_member(value, mask):
    members = 2 * lax.axis_size("seq")
    count = lax.axis_size("batch") * lax.axis_size("seq")
    return lax.ppermute(
        value,
        ("batch", "seq"),
        [(i, (i // members) * members + ((i % members) ^ mask)) for i in range(count)],
    )


def after(value, *others):
    return lax.optimization_barrier((value,) + others)[0]


def sort_blocks(value, axis, me):
    count = value.shape[axis]
    before, behind = value.shape[:axis], value.shape[axis + 1 :]
    bit = 1
    while bit < count:
        paired = value.reshape(before + (count // (2 * bit), 2, bit) + behind)
        flipped = jnp.flip(paired, axis + 1)
        value = jnp.where((me & bit) > 0, flipped, paired).reshape(value.shape)
        bit = 2 * bit
    return value


def busy(micros):
    return pl.CostEstimate(flops=0, bytes_accessed=int(micros * 3.5e6), transcendentals=0)


def far_groups(chunk):
    groups = lax.axis_size("batch") // 2
    return jnp.stack([chunk] + [swap_batch(chunk, 4 * k) for k in range(1, groups // 2)])


def near_groups(stack):
    return swap_batch(stack, 2)


def fold_near(send, keep):
    return send.shape[0], keep, swap_batch(send, 2), send.dtype


def fold_far(state, *others):
    half, keep, got, dtype = state
    total = keep[0].astype(F32) + got[0].astype(F32)
    for k in range(1, half):
        piece = (keep[k].astype(F32) + got[k].astype(F32)).astype(dtype)
        total = total + swap_batch(after(piece, *others), 4 * k).astype(F32)
    return total


def member():
    return (lax.axis_index("batch") % 2) * lax.axis_size("seq") + lax.axis_index("seq")


def exchange_members(pieces):
    me = member()
    out = jnp.zeros_like(pieces)
    for k in range(pieces.shape[0]):
        piece = lax.dynamic_index_in_dim(pieces, me ^ k, 0, keepdims=True)
        got = piece if k == 0 else swap_member(piece, k)
        out = lax.dynamic_update_slice_in_dim(out, got, me ^ k, 0)
    return out


def gather_merger(block):
    seq = lax.axis_size("seq")
    batch = lax.axis_size("batch")
    members = 2 * seq
    groups = batch // 2
    lows = groups // members
    every = ("batch", "seq")
    group = lax.axis_index("batch") // 2
    root = group // lows
    found = jnp.where(member() == root, block, jnp.zeros_like(block))
    for k in range(1, members):
        pairs = [
            (g * members + g // lows, (g ^ (k * lows)) * members + g // lows) for g in range(groups)
        ]
        found = found + lax.ppermute(block, every, pairs)
    whole = found[None]
    bit = 1
    while bit < lows:
        got = swap_batch(whole, 2 * bit)
        swapped = (group & bit) > 0
        whole = jnp.where(swapped, jnp.concatenate([got, whole]), jnp.concatenate([whole, got]))
        bit = 2 * bit
    return whole.reshape(-1, block.shape[1])


def far_tokens(value, *others):
    if lax.axis_size("seq") == 2:
        return jnp.concatenate([value, swap_seq(after(value, *others), 1)], 1)
    return lax.all_gather(value, "seq", axis=1, tiled=True)


def near_tokens(value, *others):
    seqs = value.shape[0] // 2
    return value[:seqs].astype(F32) + swap_batch(value[seqs:], 1).astype(F32)


def part_tokens(mine, *others):
    if lax.axis_size("seq") == 2:
        stretch = mine.shape[1] // 2
        return mine[:, :stretch] + swap_seq(after(mine[:, stretch:].astype(BF), *others), 1).astype(F32)
    return lax.psum_scatter(mine.astype(BF), "seq", scatter_dimension=1, tiled=True).astype(F32)


def reduce_merger(grad):
    seq = lax.axis_size("seq")
    batch = lax.axis_size("batch")
    members = 2 * seq
    groups = batch // 2
    lows = groups // members
    every = ("batch", "seq")
    group = lax.axis_index("batch") // 2
    root = group // lows
    me = member()
    whole = grad.reshape((lows, -1, grad.shape[1]))
    bit = lows // 2
    while bit:
        halves = whole.reshape((2, -1) + whole.shape[1:])
        side = ((group & bit) > 0).astype(jnp.int32)
        away = lax.dynamic_index_in_dim(halves, 1 - side, 0, keepdims=False).astype(BF)
        whole = lax.dynamic_index_in_dim(halves, side, 0, keepdims=False)
        whole = whole + swap_batch(away, 2 * bit).astype(F32)
        bit = bit // 2
    block = whole[0].astype(BF)
    total = whole[0]
    for k in range(1, members):
        pairs = [
            ((g ^ (k * lows)) * members + g // lows, g * members + g // lows) for g in range(groups)
        ]
        total = total + lax.ppermute(block, every, pairs).astype(F32)
    rows = total.reshape(members, -1, grad.shape[1]).astype(BF)
    mine = lax.dynamic_index_in_dim(rows, me, 0, keepdims=False).astype(F32)
    out = jnp.where(me == root, mine, jnp.zeros_like(mine))
    for k in range(1, members):
        pairs = [
            (g * members + g // lows, g * members + ((g // lows) ^ k)) for g in range(groups)
        ]
        piece = lax.dynamic_index_in_dim(rows, me ^ k, 0, keepdims=False)
        out = out + lax.ppermute(piece, every, pairs).astype(F32)
    return out


def centre(rows):
    mean = jnp.mean(rows, -1, keepdims=True)
    centered = rows - mean
    spread = jnp.mean(centered * centered, -1, keepdims=True)
    rstd = lax.rsqrt(spread + EPS)
    return centered * rstd, rstd


def lay(far, near, out_ref, info, parts):
    group, me = info[0], info[2]
    half = far.shape[0]
    rows = out_ref.shape[0] // (2 * half)
    small = rows // parts
    for k in range(2 * half):
        source = (far, near)[k % 2]
        for r in range(parts):
            start = (group ^ k) * rows
            if parts > 1:
                start = start + (me ^ r) * small
            start = pl.multiple_of(start, small)
            out_ref[pl.ds(start, small), :] = source[k // 2, r * small : (r + 1) * small, :]


def split_out(total_ref, send_ref, keep_ref, info, parts):
    group, me = info[0], info[2]
    half, rows, _ = send_ref.shape
    small = rows // parts
    for k in range(2 * half):
        target = (keep_ref, send_ref)[k % 2]
        for r in range(parts):
            start = (group ^ k) * rows
            if parts > 1:
                start = start + (me ^ r) * small
            start = pl.multiple_of(start, small)
            target[k // 2, r * small : (r + 1) * small, :] = total_ref[pl.ds(start, small), :].astype(BF)


def add_to(total_ref, i, value):
    @pl.when(i == 0)
    def _():
        total_ref[...] = value

    @pl.when(i > 0)
    def _():
        total_ref[...] += value


def add_rows(out_ref, i, value):
    add_to(out_ref, i, jnp.sum(value, 0, keepdims=True))


def pick(own, peer):
    return jnp.where(pl.program_id(0) < pl.num_programs(0) // 2, own[...], peer[...])


def whole(shape):
    return pl.BlockSpec(shape, lambda *_: (0,) * len(shape), pipeline_mode=pl.Buffered(1))


def tiles(rows):
    block = min(512, rows)
    steps = 2 * rows // block

    def own(n):
        return pl.BlockSpec((block, n), lambda i, *_: (jnp.minimum(i, steps // 2 - 1), 0))

    def peer(n):
        return pl.BlockSpec((block, n), lambda i, *_: (jnp.maximum(i - steps // 2, 0), 0))

    def every(n):
        return pl.BlockSpec((block, n), lambda i, *_: (i, 0))

    return block, steps, own, peer, every


def call(kernel, micros, steps, in_specs, out_specs, out_shape, scratch, *operands):
    return pl.pallas_call(
        kernel,
        grid_spec=pltpu.PrefetchScalarGridSpec(
            num_scalar_prefetch=1, grid=(steps,), in_specs=in_specs, out_specs=out_specs, scratch_shapes=scratch
        ),
        out_shape=out_shape,
        cost_estimate=busy(micros),
        compiler_params=pltpu.CompilerParams(vmem_limit_bytes=58 * 1024 * 1024),
    )(*operands)


def cut_kernel(counts, info, mixer_ref, widen_ref, merger_ref, small_ref, *outs):
    members, groups, slim, unit = counts
    share, wide = mixer_ref.shape
    width = wide // 3
    start = 3 * slim + groups * unit
    for r, out in enumerate(outs):
        t = info[2] ^ r
        for c in range(3):
            columns = pl.ds(pl.multiple_of(c * width + t * slim, slim), slim)
            out[:share, c * slim : (c + 1) * slim] = mixer_ref[:, columns]
        for g in range(groups):
            columns = pl.ds(pl.multiple_of((g * members + t) * unit, unit), unit)
            out[:share, 3 * slim + g * unit : 3 * slim + (g + 1) * unit] = widen_ref[:, columns]
        out[:share, start:] = merger_ref[...]
        out[share:, :] = small_ref[...]


def cut_pieces(counts, info, mixer, widen, merger, small):
    members = counts[0]
    shape = (mixer.shape[0] + small.shape[0], small.shape[1])
    return call(
        functools.partial(cut_kernel, counts),
        3,
        1,
        [whole(mixer.shape), whole(widen.shape), whole(merger.shape), whole(small.shape)],
        [whole(shape)] * members,
        [jax.ShapeDtypeStruct(shape, BF)] * members,
        [],
        info, mixer, widen, merger, small,
    )


def paste_kernel(counts, info, *refs):
    members, lead, unit = counts
    parts, out = refs[:members], refs[members]
    for r, part in enumerate(parts):
        t = info[2] ^ r
        for g in range(lead):
            columns = pl.ds(pl.multiple_of((g * members + t) * unit, unit), unit)
            out[:, columns] = part[:, g * unit : (g + 1) * unit].astype(F32)


def paste_columns(info, parts, lead):
    members = len(parts)
    rows, columns = parts[0].shape
    shape = (rows, members * columns)
    return call(
        functools.partial(paste_kernel, (members, lead, columns // lead)),
        2,
        1,
        [whole(part.shape) for part in parts],
        whole(shape),
        jax.ShapeDtypeStruct(shape, F32),
        [],
        info, *parts,
    )


def swap_pieces(pieces):
    return [pieces[0]] + [swap_member(piece, k) for k, piece in enumerate(pieces) if k]


def sum_all(value):
    count = lax.axis_size("batch")
    bit = count // 2
    while bit:
        value = value + swap_batch(value, bit)
        bit = bit // 2
    bit = lax.axis_size("seq") // 2
    while bit:
        value = value + swap_seq(value, bit)
        bit = bit // 2
    return value


def attend_kernel(heads, block, info, q_ref, k_ref, v_ref, g_ref, c_ref, s_ref, begin_ref, mixed_ref, grad_ref):
    length = q_ref.shape[0]
    half = ROT // 2
    cosine, sine = c_ref[0], s_ref[0]
    middle = length // 2
    low = pl.ds(pl.multiple_of(info[1] * middle, middle), middle)
    high = pl.ds(pl.multiple_of((1 - info[1]) * middle, middle), middle)

    def take(ref):
        return jnp.concatenate([ref[low, :], ref[high, :]], 0)

    def put(ref, value):
        ref[low, :] = value[:middle]
        ref[high, :] = value[middle:]

    def put_grad(part, value):
        grad_ref[part, low, :] = value[:middle]
        grad_ref[part, high, :] = value[middle:]

    lane = lax.broadcasted_iota(jnp.int32, cosine.shape, 1) % HD
    leading = lane < half

    def roll(value, shift):
        if value.shape[1] % 128:
            return jnp.concatenate([value[:, -shift:], value[:, :-shift]], 1)
        return pltpu.roll(value, shift % value.shape[1], 1)

    def turn(value):
        return value * cosine + jnp.where(leading, -roll(value, -half), roll(value, half)) * sine

    def turn_back(value):
        return value * cosine + jnp.where(leading, roll(value, -half), -roll(value, half)) * sine

    keys_f = turn(take(k_ref))
    values_f = take(v_ref)
    query = (turn(take(q_ref)).astype(BF).astype(F32) * SCALE).astype(BF)
    keys, values = keys_f.astype(BF), values_f.astype(BF)
    keys_t, values_t = keys_f.T.astype(BF), values_f.T.astype(BF)
    grads = take(g_ref)
    grads_t = grads.astype(F32).T
    begin = begin_ref[0]
    dq_all, dk_all, dv_all, mixed_all = [], [], [], []
    for h in range(heads):
        span = slice(h * HD, (h + 1) * HD)
        qh, kh, vh, gh = query[:, span], keys[:, span], values[:, span], grads[:, span]
        kt, vt, gt = keys_t[span], values_t[span], grads_t[span]
        dq_parts, mixed_parts = [], []
        dk = [jnp.zeros((block, HD), F32) for _ in range(length // block)]
        dv = [jnp.zeros((block, HD), F32) for _ in range(length // block)]
        for i in range(length // block):
            n = (i + 1) * block
            rows = slice(i * block, n)
            q, g = qh[rows], gh[rows]
            scores = dot(kh[:n], q, 1, 1)
            place_k = lax.broadcasted_iota(jnp.int32, (n, block), 0)
            place_q = lax.broadcasted_iota(jnp.int32, (n, block), 1) + i * block
            allowed = (place_k >= begin[:, rows]) & (place_k <= place_q)
            scores = jnp.where(allowed, scores, -1e30)
            expo = jnp.exp(scores - jnp.max(scores, 0, keepdims=True))
            prob = expo * (1.0 / jnp.sum(expo, 0, keepdims=True))
            prob_b = prob.astype(BF)
            mixed = dot(vt[:, :n], prob_b, 1, 0)
            mixed_parts.append(mixed)
            center = jnp.sum(mixed * gt[:, rows], 0, keepdims=True)
            score_grad = (prob * (dot(vh[:n], g, 1, 1) - center)).astype(BF)
            dq_parts.append(dot(kt[:, :n], score_grad, 1, 0) * SCALE)
            dk_add = dot(score_grad, q, 1, 0)
            dv_add = dot(prob_b, g, 1, 0)
            for j in range(i + 1):
                dk[j] = dk[j] + dk_add[j * block : (j + 1) * block]
                dv[j] = dv[j] + dv_add[j * block : (j + 1) * block]
        dq_all.append(jnp.concatenate(dq_parts, 1))
        mixed_all.append(jnp.concatenate(mixed_parts, 1))
        dk_all.append(jnp.concatenate(dk, 0))
        dv_all.append(jnp.concatenate(dv, 0))
    put(mixed_ref, jnp.concatenate(mixed_all, 0).T.astype(BF))
    put_grad(0, turn_back(jnp.concatenate(dq_all, 0).T).astype(BF))
    put_grad(1, turn_back(jnp.concatenate(dk_all, 1)).astype(BF))
    put_grad(2, jnp.concatenate(dv_all, 1).astype(BF))


def attend(info, side, project, mixed_grad, tables, begin):
    seqs, length = begin.shape
    seqs = seqs // 2
    skip = side * seqs
    wide = project.shape[1]
    rows = seqs * length
    width = wide // 3
    heads = min(2, width // HD)
    lanes = heads * HD
    steps = width // lanes
    block = min(256, length)

    parts = (project, project, project)
    ahead = steps
    if lanes % 128:
        parts = tuple(jnp.split(project, 3, 1))
        ahead = 0

    def of(part):
        return pl.BlockSpec((length, lanes), lambda s, h, _: (s + skip, part * ahead + h))

    table = pl.BlockSpec((1, length, lanes), lambda s, h, _: (s + skip, 0, 0))
    return pl.pallas_call(
        functools.partial(attend_kernel, heads, block),
        grid_spec=pltpu.PrefetchScalarGridSpec(
            num_scalar_prefetch=1,
            grid=(seqs, steps),
            in_specs=[
                of(0),
                of(1),
                of(2),
                of(0),
                table,
                table,
                pl.BlockSpec((1, 1, length), lambda s, h, _: (s + skip, 0, 0)),
            ],
            out_specs=[
                pl.BlockSpec((length, lanes), lambda s, h, _: (s, h)),
                pl.BlockSpec((3, length, lanes), lambda s, h, _: (0, s, h)),
            ],
        ),
        out_shape=[
            jax.ShapeDtypeStruct((rows, width), BF),
            jax.ShapeDtypeStruct((3, rows, width), BF),
        ],
        cost_estimate=busy(10 * seqs * steps),
        compiler_params=pltpu.CompilerParams(vmem_limit_bytes=56 * 1024 * 1024),
    )(info, *parts, mixed_grad, *tables, begin[:, None, :])


def project_kernel(parts, info, xo_ref, xp_ref, gm_ref, sm_ref, gf_ref, sf_ref, bias_ref, far_ref, near_ref, *refs):
    first_ref, second_ref, normed_ref, project_ref, mixer = refs

    @pl.when(pl.program_id(0) == 0)
    def _():
        lay(far_ref, near_ref, mixer, info, parts)

    normed, _ = centre(pick(xo_ref, xp_ref).astype(F32))
    first = (normed * gm_ref[...] + sm_ref[...]).astype(BF)
    first_ref[...] = first
    second_ref[...] = (normed * gf_ref[...] + sf_ref[...]).astype(BF)
    normed_ref[...] = normed.astype(BF)
    project_ref[...] = dot(first, mixer[...], 1, 0) + bias_ref[...]


def project_all(parts, info, inputs, gain, shift, gain_f, shift_f, bias, far, near):
    rows, width = inputs[0].shape
    wide = far.shape[2]
    _, steps, own, peer, every = tiles(rows)
    return call(
        functools.partial(project_kernel, parts),
        12,
        steps,
        [own(width), peer(width)] + [whole((1, width))] * 4 + [whole((1, wide))]
        + [whole(far.shape), whole(near.shape)],
        [every(width), every(width), every(width), every(wide)],
        [jax.ShapeDtypeStruct((2 * rows, width), BF)] * 3 + [jax.ShapeDtypeStruct((2 * rows, wide), F32)],
        [pltpu.VMEM((width, wide), BF)],
        info, *inputs, gain, shift, gain_f, shift_f, bias, far, near,
    )


def spread_kernel(info, go_ref, gp_ref, merger_ref, out_ref):
    out_ref[...] = dot(pick(go_ref, gp_ref), merger_ref[...], 1, 1).astype(BF)


def spread_back(info, upstream, merger):
    rows, width = upstream[0].shape
    slim = merger.shape[0]
    _, steps, own, peer, every = tiles(rows)
    return call(
        spread_kernel,
        4,
        steps,
        [own(width), peer(width), whole(merger.shape)],
        every(slim),
        jax.ShapeDtypeStruct((2 * rows, slim), BF),
        [],
        info, *upstream, merger,
    )


def widen_kernel(parts, info, second_ref, go_ref, gp_ref, bias_ref, far_ref, near_ref, *refs):
    active_ref, slope_ref, send_ref, keep_ref, widen, total = refs
    i = pl.program_id(0)
    hidden = widen.shape[1]
    piece = min(256, hidden)

    @pl.when(i == 0)
    def _():
        lay(far_ref, near_ref, widen, info, parts)
        total[...] = jnp.zeros_like(total)

    second = second_ref[...]
    upstream = pick(go_ref, gp_ref)

    def front(n):
        return dot(second, widen[:, n : n + piece], 1, 0) + bias_ref[:, n : n + piece]

    ahead = front(0)
    for n in range(0, hidden, piece):
        widened = ahead
        if n + piece < hidden:
            ahead = front(n + piece)
        bell = 0.5 + 0.5 * lax.erf(widened * (0.5**0.5))
        active = (widened * bell).astype(BF)
        slope = bell + widened * jnp.exp(-0.5 * widened * widened) * (0.15915494309189535**0.5)
        active_ref[:, n : n + piece] = active
        slope_ref[:, n : n + piece] = slope.astype(BF)
        total[n : n + piece, :] += dot(active, upstream, 0, 0)

    @pl.when(i == pl.num_programs(0) - 1)
    def _():
        split_out(total, send_ref, keep_ref, info, 1)


def narrow_kernel(parts, info, second_ref, normed_ref, go_ref, gp_ref, a_ref, s_ref, gain_ref, *refs):
    wf_ref, wn_ref, nf_ref, nn_ref, out_ref, e_ref, sums_ref, bsum_ref, send_ref, keep_ref, widen, narrow, total = refs
    i = pl.program_id(0)
    width, hidden = widen.shape
    piece = min(256, hidden)

    @pl.when(i == 0)
    def _():
        lay(wf_ref, wn_ref, widen, info, parts)
        lay(nf_ref, nn_ref, narrow, info, 1)
        total[...] = jnp.zeros_like(total)

    second = second_ref[...]
    upstream = pick(go_ref, gp_ref)
    out_ref[...] = dot(a_ref[...], narrow[...], 1, 0).astype(BF)
    grads = []
    for n in range(0, hidden, piece):
        active_grad = dot(upstream, narrow[n : n + piece, :], 1, 1)
        widened_grad = (active_grad * s_ref[:, n : n + piece].astype(F32)).astype(BF)
        grads.append(widened_grad)
        total[:, n : n + piece] += dot(second, widened_grad, 0, 0)
    widened_grad = jnp.concatenate(grads, 1)
    add_rows(bsum_ref, i, widened_grad.astype(F32))
    sums = []
    step = min(256, width)
    for n in range(0, width, step):
        second_grad = dot(widened_grad, widen[n : n + step, :], 1, 1)
        e_ref[:, n : n + step] = (second_grad * gain_ref[:, n : n + step]).astype(BF)
        product = second_grad * normed_ref[:, n : n + step].astype(F32)
        sums.append(jnp.concatenate([jnp.sum(product, 0, keepdims=True), jnp.sum(second_grad, 0, keepdims=True)], 0))
    add_to(sums_ref, i, jnp.concatenate(sums, 1))

    @pl.when(i == pl.num_programs(0) - 1)
    def _():
        split_out(total, send_ref, keep_ref, info, parts)


def feed_widen(parts, info, second, upstream, bias, far, near):
    rows, width = upstream[0].shape
    half, _, hidden = far.shape
    _, steps, own, peer, every = tiles(rows)
    shape = (half, hidden // (2 * half), width)
    return call(
        functools.partial(widen_kernel, parts),
        15,
        steps,
        [every(width), own(width), peer(width), whole((1, hidden)), whole(far.shape), whole(near.shape)],
        [every(hidden), every(hidden), whole(shape), whole(shape)],
        [jax.ShapeDtypeStruct((2 * rows, hidden), BF)] * 2 + [jax.ShapeDtypeStruct(shape, BF)] * 2,
        [pltpu.VMEM((width, hidden), BF), pltpu.VMEM((hidden, width), F32)],
        info, second, *upstream, bias, far, near,
    )


def feed_narrow(parts, info, second, normed, upstream, active, slope, gain, widen, narrow):
    rows, width = upstream[0].shape
    half, _, hidden = widen[0].shape
    _, steps, own, peer, every = tiles(rows)
    shape = (half, width // (2 * half), hidden)
    return call(
        functools.partial(narrow_kernel, parts),
        25,
        steps,
        [every(width), every(width), own(width), peer(width), every(hidden), every(hidden), whole((1, width))]
        + [whole(part.shape) for part in widen + narrow],
        [every(width), every(width), whole((2, width)), whole((1, hidden)), whole(shape), whole(shape)],
        [
            jax.ShapeDtypeStruct((2 * rows, width), BF),
            jax.ShapeDtypeStruct((2 * rows, width), BF),
            jax.ShapeDtypeStruct((2, width), F32),
            jax.ShapeDtypeStruct((1, hidden), F32),
            jax.ShapeDtypeStruct(shape, BF),
            jax.ShapeDtypeStruct(shape, BF),
        ],
        [pltpu.VMEM((width, hidden), BF), pltpu.VMEM((hidden, width), BF), pltpu.VMEM((width, hidden), F32)],
        info, second, normed, *upstream, active, slope, gain, *widen, *narrow,
    )


def merge_kernel(info, m_ref, go_ref, gp_ref, f_ref, w_ref, out_ref, grad_ref):
    mixed = m_ref[...]
    out_ref[...] = (dot(mixed, w_ref[...], 1, 0) + f_ref[...].astype(F32)).astype(BF)
    add_to(grad_ref, pl.program_id(0), dot(mixed, pick(go_ref, gp_ref), 0, 0))


def merge(info, mixed, upstream, partial, merger):
    rows, width = upstream[0].shape
    slim = mixed.shape[1]
    _, steps, own, peer, every = tiles(rows)
    return call(
        merge_kernel,
        7,
        steps,
        [every(slim), own(width), peer(width), every(width), whole(merger.shape)],
        [every(width), whole((slim, width))],
        [jax.ShapeDtypeStruct((2 * rows, width), BF), jax.ShapeDtypeStruct((slim, width), F32)],
        [],
        info, mixed, *upstream, partial, merger,
    )


def mixer_kernel(parts, info, first_ref, normed_ref, e_ref, p_ref, gain_ref, far_ref, near_ref, *refs):
    out_ref, sums_ref, bsum_ref, send_ref, keep_ref, mixer, total = refs
    i = pl.program_id(0)
    width = mixer.shape[0]

    @pl.when(i == 0)
    def _():
        lay(far_ref, near_ref, mixer, info, parts)
        total[...] = jnp.zeros_like(total)

    grad = jnp.concatenate([p_ref[0], p_ref[1], p_ref[2]], 1)
    total[...] += dot(first_ref[...], grad, 0, 0)
    sums = []
    step = min(256, width)
    for n in range(0, width, step):
        first_grad = dot(grad, mixer[n : n + step, :], 1, 1)
        e = e_ref[:, n : n + step].astype(F32)
        out_ref[:, n : n + step] = (first_grad * gain_ref[:, n : n + step] + e).astype(BF)
        product = first_grad * normed_ref[:, n : n + step].astype(F32)
        sums.append(jnp.concatenate([jnp.sum(product, 0, keepdims=True), jnp.sum(first_grad, 0, keepdims=True)], 0))
    add_to(sums_ref, i, jnp.concatenate(sums, 1))
    add_rows(bsum_ref, i, grad.astype(F32))

    @pl.when(i == pl.num_programs(0) - 1)
    def _():
        split_out(total, send_ref, keep_ref, info, parts)


def mixer_back(parts, info, first, normed, error, grads, gain, far, near):
    rows, width = first.shape
    half, _, wide = far.shape
    block, steps, own, peer, every = tiles(rows // 2)
    shape = (half, width // (2 * half), wide)
    return call(
        functools.partial(mixer_kernel, parts),
        14,
        steps,
        [every(width), every(width), every(width)]
        + [pl.BlockSpec((3, block, wide // 3), lambda i, _: (0, i, 0)), whole((1, width))]
        + [whole(far.shape), whole(near.shape)],
        [every(width), whole((2, width)), whole((1, wide)), whole(shape), whole(shape)],
        [
            jax.ShapeDtypeStruct((rows, width), BF),
            jax.ShapeDtypeStruct((2, width), F32),
            jax.ShapeDtypeStruct((1, wide), F32),
            jax.ShapeDtypeStruct(shape, BF),
            jax.ShapeDtypeStruct(shape, BF),
        ],
        [pltpu.VMEM((width, wide), BF), pltpu.VMEM((width, wide), F32)],
        info, first, normed, error, grads, gain, far, near,
    )


def turn_tables(position, lanes):
    half = ROT // 2
    lane = jnp.arange(lanes) % HD
    freq = 10000.0 ** (-((lane % half).astype(F32) * 2.0) / float(ROT))
    freq = jnp.where(lane < ROT, freq, 0.0)
    phase = position.astype(F32)[..., None] * freq
    return jnp.cos(phase), jnp.sin(phase)


def local(
    tokens,
    segments,
    cotangent,
    mixer_gain,
    mixer_shift,
    mixer_weight,
    mixer_bias,
    merger_weight,
    merger_bias,
    feeder_gain,
    feeder_shift,
    widen_weight,
    widen_bias,
    narrow_weight,
    narrow_bias,
):
    seqs, stretch, width = tokens.shape
    seq = lax.axis_size("seq")
    groups = lax.axis_size("batch") // 2
    members = 2 * seq
    devices = groups * members
    length = stretch * seq
    here = lax.axis_index("seq")
    me = member()
    group = lax.axis_index("batch") // 2
    share = mixer_weight.shape[0]
    hidden = widen_weight.shape[1]
    slim = width // members
    unit = hidden // devices
    mine_h = groups * unit
    block = members * share
    wide = 3 * slim
    turned = here if seq == 2 else jnp.zeros_like(here)
    info = jnp.stack([group, turned, me]).astype(jnp.int32)
    related = share % 16 == 0 and unit % 128 == 0 and slim % 128 == 0
    parts = members if related else 1

    vectors = (mixer_gain, mixer_shift, mixer_bias, merger_bias, feeder_gain, feeder_shift, widen_bias, narrow_bias)
    sizes = [v.shape[0] for v in vectors]
    cuts = [sum(sizes[: i + 1]) for i in range(len(sizes) - 1)]
    count = sum(sizes)
    span = wide + mine_h + width
    packed = jnp.concatenate(vectors)
    small = jnp.stack(
        [
            jnp.pad(packed, (0, span - packed.size)),
            jnp.pad(segments.reshape(-1).astype(BF), (0, span - segments.size)),
        ]
    )
    small = jnp.pad(small, ((0, 14), (0, 0)))
    if related:
        got = swap_pieces(
            cut_pieces((members, groups, slim, unit), info, mixer_weight, widen_weight, merger_weight, small)
        )
        rows_in = [piece[:share] for piece in got]
        notes = sort_blocks(jnp.stack([piece[share : share + 2] for piece in got]), 0, me)
    else:
        mixer_pieces = mixer_weight.reshape(share, 3, members, slim).transpose(2, 0, 1, 3)
        widen_pieces = widen_weight.reshape(share, groups, members, unit).transpose(2, 0, 1, 3)
        pieces = [
            mixer_pieces.reshape(members, share, wide),
            widen_pieces.reshape(members, share, mine_h),
            jnp.broadcast_to(merger_weight, (members, share, width)),
        ]
        pieces = jnp.concatenate(
            [jnp.concatenate(pieces, 2), jnp.broadcast_to(small[:2], (members, 2, span))], 1
        )
        got = exchange_members(pieces)
        rows_in = [got[t, :share] for t in range(members)]
        notes = got[:, share:]
    segs = notes[:, 1, : segments.size].astype(jnp.int32).reshape(2, seq, seqs, stretch)
    segs = segs.transpose(0, 2, 1, 3).reshape(2, seqs, length)
    segs = jnp.where(lax.axis_index("batch") % 2 == 0, segs, segs[::-1]).reshape(2 * seqs, length)
    notes = jnp.pad(notes[:, 0, :wide], ((0, (-members) % 16), (0, 0)))
    mixer_chunk = jnp.concatenate([piece[:, :wide] for piece in rows_in] + [notes], 0)
    widen_chunk = jnp.concatenate([piece[:, wide : wide + mine_h] for piece in rows_in], 0)
    merger_block = jnp.concatenate([piece[:, wide + mine_h :] for piece in rows_in], 0)

    mixer_far = far_groups(mixer_chunk)
    inputs_own = far_tokens(tokens, *got).reshape(-1, width)
    merger = gather_merger(merger_block)
    if related:
        merger = sort_blocks(merger.reshape(-1, members, share, width), 1, me).reshape(slim, width)
    mixer_near = near_groups(mixer_far)
    widen_far = far_groups(after(widen_chunk, mixer_far))
    inputs = (inputs_own, swap_batch(inputs_own, 1))
    upstream_own = far_tokens(cotangent, inputs_own).reshape(-1, width)
    upstream = (upstream_own, swap_batch(upstream_own, 1))
    widen_near = near_groups(after(widen_far, mixer_near))
    narrow_far = far_groups(after(narrow_weight, widen_far))
    narrow_near = near_groups(after(narrow_far, widen_near))
    widen = (widen_far, widen_near)
    narrow = (narrow_far, narrow_near)

    both = jnp.stack([mixer_far[:, block : block + members], mixer_near[:, block : block + members]], 1)
    gathered = sort_blocks(both.reshape(groups, members, -1)[:, :, :count], 0, group)
    gathered = gathered.reshape(devices, -1).astype(F32)
    gain_m, shift_m, bias_m, bias_o, gain_f, shift_f, bias_w, bias_n = [
        v.reshape(1, -1) for v in jnp.split(gathered, cuts, 1)
    ]
    bias_m_mine = lax.dynamic_index_in_dim(bias_m.reshape(3, members, slim), me, 1).reshape(1, -1)
    bias_w_mine = lax.dynamic_index_in_dim(bias_w.reshape(groups, members, unit), me, 1).reshape(1, -1)
    place = jnp.arange(length, dtype=jnp.int32)
    begin = jnp.sum((segs[:, None, :] < segs[:, :, None]).astype(jnp.int32), -1)
    tables = turn_tables(place[None, :] - begin, min(2, slim // HD) * HD)

    first, second, normed, project = project_all(
        parts, info, inputs, gain_m, shift_m, gain_f, shift_f, bias_m_mine, mixer_far, mixer_near
    )
    mixed_grad = spread_back(after(info, project), upstream, merger)
    mixed_a, grad_a = attend(info, 0, project, mixed_grad, tables, begin)

    active, slope, n_send, n_keep = feed_widen(
        parts, after(info, mixed_a, narrow_far), second, upstream, bias_w_mine, widen_far, widen_near
    )
    narrow_state = fold_near(n_send, n_keep)

    mixed_b, grad_b = attend(after(info, active), 1, project, mixed_grad, tables, begin)

    partial, error, feed_sums, widen_bias_grad, w_send, w_keep = feed_narrow(
        parts, after(info, mixed_b, narrow_state[2]), second, normed, upstream, active, slope, gain_f, widen, narrow
    )
    narrow_out = fold_far(narrow_state)
    widen_state = fold_near(after(w_send, narrow_state[2]), w_keep)

    mixed = jnp.concatenate([mixed_a, mixed_b], 0)
    project_grad = jnp.concatenate([grad_a, grad_b], 1)
    partial, merger_grad = merge(info, mixed, upstream, partial, merger)
    error, mixer_sums, mixer_bias_grad, m_send, m_keep = mixer_back(
        parts, after(info, partial), first, normed, error, project_grad, gain_m, mixer_far, mixer_near
    )
    own = tokens.astype(F32)
    layer_output = part_tokens(near_tokens(partial.reshape(2 * seqs, length, width)))
    mixer_state = fold_near(after(m_send, widen_state[2]), m_keep)
    widen_sum = fold_far(widen_state, narrow_out)
    merger_out = reduce_merger(merger_grad)
    mixer_sum = fold_far(mixer_state, widen_sum)

    def bring_back(total, lead):
        if related:
            got = swap_pieces([total[r * share : (r + 1) * share].astype(BF) for r in range(members)])
            return paste_columns(info, got, lead)
        got = exchange_members(total.reshape(members, share, -1).astype(BF))
        got = got.reshape(members, share, lead, -1).transpose(1, 2, 0, 3)
        return got.reshape(share, -1).astype(F32)

    widen_out = bring_back(widen_sum, groups)
    mixer_out = bring_back(mixer_sum, 3)

    error = part_tokens(near_tokens(error.reshape(2 * seqs, length, width)), layer_output)
    layer_output = (own + layer_output + (bias_o + bias_n)).astype(BF)
    normed, rstd = centre(own)
    back = rstd * (
        error
        - jnp.mean(error, -1, keepdims=True)
        - normed * jnp.mean(error * normed, -1, keepdims=True)
    )
    tokens_grad = (cotangent.astype(F32) + back).astype(BF)

    def spread_out(value, lead):
        mine = jnp.arange(members)[None, :, None] == me
        return jnp.where(mine, value.reshape(lead, 1, -1), 0.0).reshape(-1, width)

    bias_grad = jnp.sum(cotangent.astype(F32), (0, 1))[None]
    sums = (mixer_sums, spread_out(mixer_bias_grad, 3), bias_grad, feed_sums, spread_out(widen_bias_grad, groups))
    total = sum_all(jnp.concatenate(sums, 0))
    flat_index = lax.axis_index("batch") * seq + here
    at = 0
    owned = []
    for size in sizes[:-1]:
        rows = size * devices // width
        owned.append(lax.dynamic_slice_in_dim(total[at : at + rows].reshape(-1), flat_index * size, size))
        at = at + rows
    gain_m_out, shift_m_out, bias_m_out, bias_o_out, gain_f_out, shift_f_out, bias_w_out = owned
    return (
        layer_output,
        tokens_grad,
        gain_m_out,
        shift_m_out,
        mixer_out,
        bias_m_out,
        merger_out,
        bias_o_out,
        gain_f_out,
        shift_f_out,
        widen_out,
        bias_w_out,
        narrow_out,
        bias_o_out,
    )


def solution(mesh):
    vector = P(("batch", "seq"))
    matrix = P(("batch", "seq"), None)
    rows = P("batch", "seq", None)
    params = (vector, vector, matrix, vector, matrix, vector, vector, vector, matrix, vector, matrix, vector)
    return jax.shard_map(
        local,
        mesh=mesh,
        in_specs=(rows, P("batch", "seq"), rows) + params,
        out_specs=(rows, rows) + params,
        check_vma=False,
    )
```
